32 devices in a mesh: grp: 2 (over y), ep: 16 (over z, x, core), tp: 1.
Axes of the slice: x: 2, y: 2, z: 4, core: 2. Of those that a mesh axis runs over, the one named last changes fastest.
Arguments:
- hidden_in: bfloat16 [2, 256, 2048], P(None, ('grp', 'ep')), parts along dimension 1, may hold values from -6 to 6
- routes: int32 [2, 256, 8], P(None, ('grp', 'ep')), parts along dimension 1, may hold values from 0 to 7, all different within a row; in each aligned block of 8 rows (0 to 7, 8 to 15, ..., all dimensions but the last counted through in order) at most 8 rows name the same one
- gates: float32 [2, 256, 8], P(None, ('grp', 'ep')), parts along dimension 1, may hold values from 0.1 to 1
- query: bfloat16 [2, 256, 8192], P(None, ('grp', 'ep'), 'tp'), parts along dimension 1, may hold values from -13 to 13
- cached_key_rows: bfloat16 [2, 256, 64, 512], P(None, ('grp', 'ep'), None, 'tp'), parts along dimension 1, may hold values from -4 to 4
- cached_value_rows: bfloat16 [2, 256, 64, 512], P(None, ('grp', 'ep'), None, 'tp'), parts along dimension 1, may hold values from -4 to 4
- fresh_key: bfloat16 [2, 256, 512], P(None, ('grp', 'ep'), 'tp'), parts along dimension 1, may hold values from -4 to 4
- fresh_value: bfloat16 [2, 256, 512], P(None, ('grp', 'ep'), 'tp'), parts along dimension 1, may hold values from -4 to 4
- lengths: int32 [2, 256], P(None, ('grp', 'ep')), parts along dimension 1, may hold values from 2 to 64, as said below
- w_gate: bfloat16 [16, 2048, 384], P('ep', None, 'tp'), may hold values from -0.125 to 0.125
- w_up: bfloat16 [16, 2048, 384], P('ep', None, 'tp'), may hold values from -0.125 to 0.125
- w_down: bfloat16 [16, 384, 2048], P('ep', 'tp'), may hold values from -0.21875 to 0.21875
Outputs:
- attn_out: bfloat16 [2, 256, 8192], P(None, ('grp', 'ep'), 'tp'), parts along dimension 1
- moe_out: bfloat16 [2, 256, 2048], P(None, ('grp', 'ep'), 'tp'), parts along dimension 1
The draws below stay inside these ranges and needn't reach their ends.
There are 2 independent parts, one for each index of `grp`. The reference program is written for one: setup_inputs(seed, part) draws one part's arguments, and reference() takes and returns one part's arrays. A program takes and returns all parts, laid end to end along the dimension named above; an argument that names none is the same for every part. Nothing has to cross between parts.
Inputs may be any that keep to these rules, and one draw needn't show every extreme that they name: `routes`: in each micro-batch no expert is named by more than 8 of the 8 rows of one index of ep, a bound that some block reaches of them; a row names 8 different experts. `lengths`: some row has all 64 positions live.
All inputs are finite; a program needn't handle non-finite values.
Results may differ from the reference program's by a relative error of at most 0.0057.
Values may be sent and summed in bfloat16 or wider, within the bound.
A program may use at most 64 MiB of HBM per device.

```python
import math
import jax
import jax.numpy as jnp
import numpy as np
from jax import lax

D = 2048
FFE = 768
QUERY_HEADS = 64
KEY_VALUE_HEADS = 4
HEAD_SIZE = 128
TOPK = 8
MICRO_BATCHES = 2
ROWS_DEV = 8
CACHE_SLOTS = 64
EXPERTS = 8
MICRO_ROWS = 128
MOST = 8
N_EP = 16


def attention_draw(key):
    base_key = jax.random.fold_in(key, 101)
    cache_random_key, query_random_key = jax.random.split(base_key, 2)
    cache_store = jnp.clip(jax.random.normal(cache_random_key, (MICRO_BATCHES, MICRO_ROWS, CACHE_SLOTS, KEY_VALUE_HEADS, HEAD_SIZE), jnp.float32), -4.0, 4.0)
    query_rows = jnp.clip(jax.random.normal(query_random_key, (MICRO_BATCHES, MICRO_ROWS, KEY_VALUE_HEADS, QUERY_HEADS // KEY_VALUE_HEADS, HEAD_SIZE), jnp.float32), -4.0, 4.0)
    return (cache_store, query_rows)


def draw_query(key, part):
    cache_store, query_rows = attention_draw(key)
    return query_rows.reshape(MICRO_BATCHES, MICRO_ROWS, QUERY_HEADS * HEAD_SIZE).astype(jnp.bfloat16)


def draw_cached_key_rows(key, part):
    cache_store, query_rows = attention_draw(key)
    return cache_store.reshape(MICRO_BATCHES, MICRO_ROWS, CACHE_SLOTS, KEY_VALUE_HEADS * HEAD_SIZE).astype(jnp.bfloat16)


def draw_lengths(key, part):
    length_key = jax.random.fold_in(key, 211)
    drawn = jax.random.randint(length_key, (MICRO_BATCHES, MICRO_ROWS), 2, CACHE_SLOTS + 1)
    marked = jnp.arange(MICRO_BATCHES * MICRO_ROWS, dtype=jnp.int32).reshape(MICRO_BATCHES, MICRO_ROWS) % 17 == 0
    return jnp.where(marked, CACHE_SLOTS, drawn).astype(jnp.int32)


def levels(own_key, extent, shards, least, largest):
    gain, own = 1.0, jax.random.fold_in(own_key, 6)
    for position, shards_of in shards:
        heights = jnp.exp(jax.random.uniform(jax.random.fold_in(own, position), (shards_of,), jnp.float32, least / len(shards), largest / len(shards)))
        gain = gain * jnp.repeat(heights, extent[position] // shards_of).reshape([-1 if axis == position else 1 for axis in range(len(extent))])
    return gain


def assign_block(key, own, number, rows, amount, top, reach, skew):
    sequence = jax.random.permutation(key, amount)
    packed, usual = load_shares(amount, rows * top, reach, skew, True), load_shares(amount, rows * top, reach, skew, False)
    places = jnp.arange(amount)

    def named(sizes, turn):
        used = int((sizes > 0).sum())
        fixed = max(1, used // 4)
        shifted = fixed + (places - fixed + turn * (used - fixed)) % max(1, amount - fixed)
        return jnp.zeros((amount,), jnp.int32).at[sequence[jnp.where(places < fixed, places, shifted)]].set(jnp.asarray(sizes, jnp.int32))

    sizes = jnp.where(number % 4 == 0, named(packed, number // 4), named(usual, number - number // 4 - 1))
    mixed = jax.random.permutation(jax.random.fold_in(own, 3), amount)
    source_of, taker = mixed[0:amount // 2 * 2:2], mixed[1:amount // 2 * 2:2]
    slack = jnp.minimum(sizes[source_of] - 1, reach - sizes[taker]) // 2
    slack = jnp.where((source_of == sequence[0]) | (taker == sequence[0]) | (sizes[taker] == 0), 0, jnp.maximum(slack, 0))
    shifted = jax.random.randint(jax.random.fold_in(own, 4), (amount // 2,), 0, 1 << 20) % (slack + 1)
    sizes = sizes.at[source_of].add(-shifted).at[taker].add(shifted)
    labels = jnp.searchsorted(jnp.cumsum(sizes), jnp.arange(rows * top), side="right").astype(jnp.int32)
    grid = labels.reshape(top, rows).T
    grid = grid[jax.random.permutation(jax.random.fold_in(own, 1), rows)]
    turn = jax.random.randint(jax.random.fold_in(own, 2), (rows, 1), 0, top)
    return jnp.take_along_axis(grid, (jnp.arange(top)[None, :] + turn) % top, axis=1)


def load_shares(amount, total, most, slope, full):
    loads = [(1 << 20) // math.isqrt(standing ** slope) + 1 for standing in range(1, amount + 1)]
    largest = most if full else min(most, max(-(-total // amount), total * loads[0] // sum(loads)))
    least = 1 if total - largest >= amount - 1 else 0
    holding, spare = [largest] + [least] * (amount - 1), total - largest - least * (amount - 1)
    while spare > 0:
        free = [i for i in range(1, amount) if holding[i] < largest] or [i for i in range(1, amount) if holding[i] < most]
        whole, left = sum([loads[i] for i in free]), spare
        for i in free:
            more = min(most - holding[i], max(1, left * loads[i] // whole), spare)
            holding[i] = holding[i] + more
            spare = spare - more
    return np.array(holding)


def centred(key, dims, width, limit, cuts=(), kind=jnp.bfloat16):
    entries = jax.random.normal(key, dims, jnp.float32) * width
    if len(cuts) > 0:
        entries = levels(key, dims, cuts, -0.22, 0.18) * entries
    return jnp.clip(entries, min=-limit, max=limit).astype(kind)


def setup_inputs(seed: int = 0, part: int = 0) -> dict:
    arg_keys = jax.random.split(jax.random.key(seed), 13)
    part_keys = jax.random.split(jax.random.fold_in(arg_keys[12], part), 13)
    hidden_in = centred(part_keys[0], (MICRO_BATCHES, MICRO_ROWS, D), 1.0, 6.0, ((1, 16),))
    routes_keys = jax.random.split(jax.random.fold_in(part_keys[1], 1), MICRO_BATCHES * MICRO_ROWS // ROWS_DEV)
    routes_turns = jax.random.permutation(jax.random.fold_in(part_keys[1], 3), MICRO_BATCHES * MICRO_ROWS // ROWS_DEV)
    routes = jax.vmap(lambda own, number: assign_block(jax.random.fold_in(part_keys[1], 2), own, number, ROWS_DEV, EXPERTS, TOPK, MOST, 2))(routes_keys, routes_turns).reshape((MICRO_BATCHES, MICRO_ROWS, TOPK))
    gates = jnp.clip(0.1 + 0.9 * jax.random.uniform(part_keys[2], (MICRO_BATCHES, MICRO_ROWS, TOPK), jnp.float32) ** levels(part_keys[2], (MICRO_BATCHES, MICRO_ROWS, TOPK), ((1, 16),), -0.2, 0.2), 0.1, 1.0)
    query = draw_query(jax.random.fold_in(jax.random.fold_in(arg_keys[12], part), 71), part)
    cached_key_rows = draw_cached_key_rows(jax.random.fold_in(jax.random.fold_in(arg_keys[12], part), 71), part)
    cached_value_rows = centred(part_keys[5], (MICRO_BATCHES, MICRO_ROWS, CACHE_SLOTS, KEY_VALUE_HEADS * HEAD_SIZE), 1.0, 4.0, ((1, 16),))
    fresh_key = centred(part_keys[6], (MICRO_BATCHES, MICRO_ROWS, KEY_VALUE_HEADS * HEAD_SIZE), 1.0, 4.0, ((1, 16),))
    fresh_value = centred(part_keys[7], (MICRO_BATCHES, MICRO_ROWS, KEY_VALUE_HEADS * HEAD_SIZE), 1.0, 4.0, ((1, 16),))
    lengths = draw_lengths(jax.random.fold_in(jax.random.fold_in(arg_keys[12], part), 71), part)
    w_gate = centred(arg_keys[9], (2 * EXPERTS, D, FFE // 2), D ** -0.5, 0.125, ((0, 16),))
    w_up = centred(arg_keys[10], (2 * EXPERTS, D, FFE // 2), D ** -0.5, 0.125, ((0, 16),))
    w_down = centred(arg_keys[11], (2 * EXPERTS, FFE // 2, D), FFE ** -0.5, 0.21875, ((0, 16),))
    return {"hidden_in": hidden_in, "routes": routes, "gates": gates, "query": query, "cached_key_rows": cached_key_rows, "cached_value_rows": cached_value_rows, "fresh_key": fresh_key, "fresh_value": fresh_value, "lengths": lengths, "w_gate": w_gate, "w_up": w_up, "w_down": w_down}


def attend_rows(query, cached_key_rows, cached_value_rows, fresh_key, fresh_value, lengths):
    row_count_total = query.shape[0]
    query_group = QUERY_HEADS // KEY_VALUE_HEADS
    grouped_query_rows = query.astype(jnp.float32).reshape(row_count_total, KEY_VALUE_HEADS, query_group, HEAD_SIZE)
    earlier_keys = cached_key_rows.astype(jnp.float32).reshape(row_count_total, CACHE_SLOTS, KEY_VALUE_HEADS, HEAD_SIZE)
    earlier_values = cached_value_rows.astype(jnp.float32).reshape(row_count_total, CACHE_SLOTS, KEY_VALUE_HEADS, HEAD_SIZE)
    token_own_keys = fresh_key.astype(jnp.float32).reshape(row_count_total, KEY_VALUE_HEADS, HEAD_SIZE)
    token_own_values = fresh_value.astype(jnp.float32).reshape(row_count_total, KEY_VALUE_HEADS, HEAD_SIZE)
    score_scale = 1.0 / math.sqrt(HEAD_SIZE)
    past_score = jnp.einsum('rkgd,rckd->rkgc', grouped_query_rows, earlier_keys) * score_scale
    own_score = jnp.einsum('rkgd,rkd->rkg', grouped_query_rows, token_own_keys)[..., None] * score_scale
    valid_pos = jnp.arange(CACHE_SLOTS, dtype=jnp.int32)[None, :] < lengths[:, None]
    past_score = jnp.where(valid_pos[:, None, None, :], past_score, -jnp.inf)
    scores = jnp.concatenate([past_score, own_score], axis=-1)
    row_max = lax.optimization_barrier(jnp.max(scores, axis=-1, keepdims=True))
    exp_scores = jnp.exp(scores - row_max)
    weights_bf = exp_scores / lax.optimization_barrier(jnp.sum(exp_scores, axis=-1, keepdims=True))
    weights_bf = lax.optimization_barrier(weights_bf.astype(jnp.bfloat16)).astype(jnp.float32)
    attended = jnp.einsum('rkgc,rckd->rkgd', weights_bf[..., :CACHE_SLOTS], earlier_values)
    attended = attended + weights_bf[..., CACHE_SLOTS:] * token_own_values[:, :, None, :]
    return attended.reshape(row_count_total, QUERY_HEADS * HEAD_SIZE).astype(jnp.bfloat16)

def expert_mix(tokens, routes, gates, w_gate, w_up, w_down):
    row_count_total = tokens.shape[0]
    down_full = w_down.reshape(EXPERTS, FFE, D)
    slot_bound = MICRO_BATCHES * N_EP * MOST

    def one_expert(accum, expert):
        matched = routes == expert
        weight = lax.optimization_barrier(jnp.sum(jnp.where(matched, gates, 0.0), axis=1))
        named = jnp.any(matched, axis=1)
        picked = jnp.nonzero(named, size=slot_bound, fill_value=0)[0].astype(jnp.int32)
        live_count = jnp.sum(named.astype(jnp.int32))
        slot_rows = tokens[picked]
        gate_val = jnp.concatenate([jnp.dot(slot_rows, w_gate[2 * expert], preferred_element_type=jnp.float32), jnp.dot(slot_rows, w_gate[2 * expert + 1], preferred_element_type=jnp.float32)], axis=1)
        up_val = jnp.concatenate([jnp.dot(slot_rows, w_up[2 * expert], preferred_element_type=jnp.float32), jnp.dot(slot_rows, w_up[2 * expert + 1], preferred_element_type=jnp.float32)], axis=1)
        hidden = (jax.nn.silu(gate_val) * up_val).astype(jnp.bfloat16)
        expert_out = jnp.dot(hidden, down_full[expert], preferred_element_type=jnp.float32).astype(jnp.bfloat16)
        expert_out = lax.optimization_barrier(expert_out).astype(jnp.float32)
        keep = (jnp.arange(slot_bound, dtype=jnp.int32) < live_count).astype(jnp.float32)
        contrib = (weight[picked] * keep)[:, None] * expert_out
        return (accum.at[picked].add(contrib), None)
    start = jnp.zeros((row_count_total, D), jnp.float32)
    accum, _ = lax.scan(one_expert, start, jnp.arange(EXPERTS, dtype=jnp.int32))
    return accum.astype(jnp.bfloat16)

def reference(hidden_in, routes, gates, query, cached_key_rows, cached_value_rows, fresh_key, fresh_value, lengths, w_gate, w_up, w_down):
    attn_list = []
    for batch_idx in range(MICRO_BATCHES):
        attn_list.append(attend_rows(query[batch_idx], cached_key_rows[batch_idx], cached_value_rows[batch_idx], fresh_key[batch_idx], fresh_value[batch_idx], lengths[batch_idx]))
    attn_out = jnp.stack(attn_list)
    mixed = expert_mix(hidden_in.reshape(MICRO_BATCHES * MICRO_ROWS, D), routes.reshape(MICRO_BATCHES * MICRO_ROWS, TOPK), gates.reshape(MICRO_BATCHES * MICRO_ROWS, TOPK), w_gate, w_up, w_down)
    moe_out = mixed.reshape(MICRO_BATCHES, MICRO_ROWS, D)
    return (attn_out, moe_out)
```

```python
import functools
import math

import jax
import jax.numpy as jnp
from jax import lax
from jax.experimental import pallas as pl
from jax.experimental.pallas import tpu as pltpu
from jax.sharding import PartitionSpec as P

QUERY_HEADS = 64
KEY_VALUE_HEADS = 4
HEAD_SIZE = 128


def swapped(block, axis, bit):
    count = lax.axis_size(axis)
    route = []
    for low in range(count):
        high = low | 1 << bit
        if high != low and high < count:
            route += [(low, high), (high, low)]
    return lax.ppermute(block, axis, route)


def attend_local(query_rows, cached_key_rows, cached_value_rows, fresh_key, fresh_value, lengths):
    row_count = query_rows.shape[0]
    query_group = QUERY_HEADS // KEY_VALUE_HEADS
    kv_local = cached_key_rows.shape[2] // HEAD_SIZE
    cache_len = cached_key_rows.shape[1]
    grouped_query_rows = query_rows.reshape(row_count, kv_local, query_group, HEAD_SIZE)
    earlier_keys = cached_key_rows.reshape(row_count, cache_len, kv_local, HEAD_SIZE)
    earlier_values = cached_value_rows.reshape(row_count, cache_len, kv_local, HEAD_SIZE)
    token_own_keys = fresh_key.reshape(row_count, kv_local, HEAD_SIZE)
    token_own_values = fresh_value.reshape(row_count, kv_local, HEAD_SIZE).astype(jnp.float32)
    score_scale = 1.0 / math.sqrt(HEAD_SIZE)
    past_score = (
        jnp.einsum(
            "rkgd,rckd->rkgc", grouped_query_rows, earlier_keys, preferred_element_type=jnp.float32
        )
        * score_scale
    )
    own_score = (
        jnp.einsum(
            "rkgd,rkd->rkg", grouped_query_rows, token_own_keys, preferred_element_type=jnp.float32
        )[..., None]
        * score_scale
    )
    valid_pos = lax.broadcasted_iota(jnp.int32, (row_count, cache_len), 1) < lengths[:, None]
    past_score = jnp.where(valid_pos[:, None, None, :], past_score, -jnp.inf)
    scores = jnp.concatenate([past_score, own_score], axis=-1)
    row_max = jnp.max(scores, axis=-1, keepdims=True)
    exp_scores = jnp.exp(scores - row_max)
    weights_bf = (exp_scores / jnp.sum(exp_scores, axis=-1, keepdims=True)).astype(jnp.bfloat16)
    attended = jnp.einsum(
        "rkgc,rckd->rkgd",
        weights_bf[..., :cache_len],
        earlier_values,
        preferred_element_type=jnp.float32,
    )
    attended = (
        attended + weights_bf[..., cache_len:].astype(jnp.float32) * token_own_values[:, :, None, :]
    )
    return attended.reshape(row_count, kv_local * query_group * HEAD_SIZE).astype(jnp.bfloat16)


def slot_layout(route_rows, experts, capacity):
    flat_routes = route_rows.reshape(-1)
    onehot = (flat_routes[:, None] == jnp.arange(experts, dtype=jnp.int32)[None, :]).astype(
        jnp.int32
    )
    before = jnp.cumsum(onehot, axis=0) - onehot
    slot_rank = jnp.sum(before * onehot, axis=1)
    return 2 * flat_routes * capacity + slot_rank


def pack_rows(tokens, first_slot, capacity, slot_total, route_count):
    targets = jnp.stack([first_slot, first_slot + capacity], axis=1)
    slot_ids = lax.broadcasted_iota(jnp.int32, (slot_total, 1, 1), 0)
    chosen = jnp.sum((targets[None, :, :] == slot_ids).astype(jnp.float32), axis=2)
    chosen = jnp.sum(chosen.reshape(slot_total, -1, route_count), axis=2).astype(jnp.bfloat16)
    return jnp.dot(chosen, tokens, preferred_element_type=jnp.float32).astype(jnp.bfloat16)


def combine_rows(returned, first_slot, capacity, row_gates, row_count, route_count):
    flat_back = returned.reshape(returned.shape[0] * returned.shape[1], returned.shape[2])
    lower = jnp.take(flat_back, first_slot, axis=0)
    upper = jnp.take(flat_back, first_slot + capacity, axis=0)
    outputs = jnp.concatenate([lower, upper], axis=1)
    outputs = lax.optimization_barrier(outputs).astype(jnp.float32)
    weighted = row_gates.reshape(-1, 1) * outputs
    return jnp.sum(weighted.reshape(row_count, route_count, -1), axis=1).astype(jnp.bfloat16)


def sparse_shards(
    hidden_in,
    routes,
    gates,
    query,
    cached_key_rows,
    cached_value_rows,
    fresh_key,
    fresh_value,
    lengths,
    w_gate,
    w_up,
    w_down,
):
    ep_size = lax.axis_size("ep")
    experts = ep_size // 2
    batches, row_count, route_count = routes.shape
    model_width = hidden_in.shape[2]
    capacity = min(row_count, 2 * ((row_count * route_count + experts - 1) // experts))
    slot_total = ep_size * capacity
    layouts = []
    buffers = []
    for batch_idx in range(batches):
        first_slot = slot_layout(routes[batch_idx], experts, capacity)
        layouts.append(first_slot)
        packed = pack_rows(hidden_in[batch_idx], first_slot, capacity, slot_total, route_count)
        buffers.append(packed.reshape(ep_size, capacity, model_width))
    attn_list = []
    blocks = []
    for batch_idx in range(batches):
        received = lax.all_to_all(buffers[batch_idx], "ep", split_axis=0, concat_axis=0, tiled=True)
        item_count = received.shape[1]
        slot_rows = received.reshape(ep_size * item_count, model_width)
        gate_val = jnp.dot(slot_rows, w_gate[0], preferred_element_type=jnp.float32)
        up_val = jnp.dot(slot_rows, w_up[0], preferred_element_type=jnp.float32)
        hidden = (jax.nn.silu(gate_val) * up_val).astype(jnp.bfloat16)
        partial_value = jnp.dot(hidden, w_down[0], preferred_element_type=jnp.float32)
        partial_value = partial_value.reshape(ep_size, item_count, model_width)
        half_sum = lax.psum_scatter(partial_value, "tp", scatter_dimension=2, tiled=True)
        partner = swapped(half_sum, "ep", 0)
        finished = (half_sum + partner).astype(jnp.bfloat16)
        quarter = finished.shape[2] // 2
        parity = lax.axis_index("ep") % 2
        quarter_cols = lax.dynamic_slice_in_dim(finished, parity * quarter, quarter, 2)
        blocks.append(lax.all_to_all(quarter_cols, "ep", split_axis=0, concat_axis=0, tiled=True))
        attn_list.append(
            attend_local(
                query[batch_idx],
                cached_key_rows[batch_idx],
                cached_value_rows[batch_idx],
                fresh_key[batch_idx],
                fresh_value[batch_idx],
                lengths[batch_idx],
            )
        )
    moe_list = []
    for batch_idx in range(batches):
        moe_list.append(
            combine_rows(
                blocks[batch_idx],
                layouts[batch_idx],
                capacity,
                gates[batch_idx],
                row_count,
                route_count,
            )
        )
    return (jnp.stack(attn_list), jnp.stack(moe_list))


LANES = 128
TILE_ROWS = 16
PAIR = 2
MESH = pl.DeviceIdType.MESH


def remote(src, dst, send_sem, recv_sem, index):
    return pltpu.make_async_remote_copy(
        src_ref=src,
        dst_ref=dst,
        send_sem=send_sem,
        recv_sem=recv_sem,
        device_id={"ep": index},
        device_id_type=MESH,
    )


def layer_kernel(
    dims,
    hidden_ref,
    routes_ref,
    gates_ref,
    query_ref,
    fresh_key_ref,
    fresh_value_ref,
    lengths_ref,
    key_hbm,
    value_hbm,
    gate_hbm,
    up_hbm,
    down_hbm,
    attn_ref,
    moe_ref,
    keys,
    values,
    w_gate,
    w_up,
    w_down,
    gathered,
    q_rows,
    o_rows,
    own_keys,
    own_values,
    row_weight,
    act,
    keep_c,
    keep_x,
    send_c,
    recv_c,
    send_x,
    recv_x,
    send_z,
    recv_z,
    load_sems,
    gz_send,
    gz_recv,
    gx_send,
    gx_recv,
    gc_send,
    gc_recv,
    rc_send,
    rc_recv,
    rx_send,
    rx_recv,
    rz_send,
    rz_recv,
):
    batches, rows, width, heads, kv_heads, slots, experts, depth, chunks, chunk = dims
    ring = gz_send.shape[0]
    block = batches * rows
    quarter = ring * block
    half = PAIR * quarter
    group = heads // kv_heads
    scale = 1.0 / math.sqrt(HEAD_SIZE)

    me = lax.axis_index("ep")
    core = lax.rem(me, PAIR)
    across = lax.rem(me // PAIR, PAIR)
    place = lax.rem(me, PAIR * PAIR)
    level = me // (PAIR * PAIR)
    mate = me + 1 - PAIR * core
    side = me + PAIR - PAIR * PAIR * across

    def up_by(step):
        return lax.rem(level + step, ring) * (PAIR * PAIR) + place

    def down_by(step):
        return lax.rem(level + ring - step, ring) * (PAIR * PAIR) + place

    loads = [
        pltpu.make_async_copy(source, target, load_sems.at[i])
        for i, (source, target) in enumerate(
            (
                (key_hbm, keys),
                (value_hbm, values),
                (gate_hbm, w_gate),
                (up_hbm, w_up),
                (down_hbm, w_down),
            )
        )
    ]
    for load in loads:
        load.start()

    barrier = pltpu.get_barrier_semaphore()
    others = [mate, side] + [up_by(step) for step in range(1, ring)]
    for other in others:
        pl.semaphore_signal(barrier, inc=1, device_id={"ep": other}, device_id_type=MESH)

    own = [hidden_ref[b].astype(jnp.float32) for b in range(batches)]
    gathered[0:block, 0:width] = jnp.concatenate(own, axis=0).astype(jnp.bfloat16)
    spread = gathered.shape[1] - width
    lane = lax.broadcasted_iota(jnp.int32, (rows, spread), 1)
    expert_of = lax.rem(lane, experts)
    tails = []
    for b in range(batches):
        dense = jnp.zeros((rows, spread), jnp.float32)
        for k in range(routes_ref.shape[2]):
            named = routes_ref[b, :, k : k + 1] == expert_of
            dense = dense + jnp.where(named, gates_ref[b, :, k : k + 1], 0.0)
        high = dense.astype(jnp.bfloat16).astype(jnp.float32)
        tail = jnp.where(lane < experts, high, dense - high)
        tails.append(jnp.where(lane < 2 * experts, tail, 0.0))
    gathered[0:block, width:] = jnp.concatenate(tails, axis=0).astype(jnp.bfloat16)

    pl.semaphore_wait(barrier, len(others))

    def slot(far_core, far_side, step):
        return pl.ds(((far_core * PAIR + far_side) * ring + step) * block, block)

    def gather_z(step):
        return remote(
            gathered.at[slot(0, 0, 0)],
            gathered.at[slot(0, 0, step)],
            gz_send.at[step],
            gz_recv.at[step],
            up_by(step),
        )

    def gather_x(step):
        return remote(
            gathered.at[slot(0, 0, step)],
            gathered.at[slot(0, 1, step)],
            gx_send.at[step],
            gx_recv.at[step],
            side,
        )

    def gather_c(far_side, step):
        return remote(
            gathered.at[slot(0, far_side, step)],
            gathered.at[slot(1, far_side, step)],
            gc_send.at[far_side * ring + step],
            gc_recv.at[far_side * ring + step],
            mate,
        )

    order = sorted(range(1, ring), key=lambda step: min(step, ring - step))
    for step in order:
        gather_z(step).start()
    gather_x(0).start()
    gather_c(0, 0).start()

    for b in range(batches):
        own_keys[b] = fresh_key_ref[b].astype(jnp.float32)
        own_values[b] = fresh_value_ref[b].astype(jnp.float32)
        for h in range(heads):
            q_rows[b, h * rows : (h + 1) * rows, :] = query_ref[
                b, :, h * HEAD_SIZE : (h + 1) * HEAD_SIZE
            ].astype(jnp.float32)
    loads[0].wait()
    loads[1].wait()

    head = lax.broadcasted_iota(jnp.int32, (heads, kv_heads * slots), 0)
    column = lax.broadcasted_iota(jnp.int32, (heads, kv_heads * slots), 1)
    position = jnp.where(head // group == column // slots, lax.rem(column, slots), slots)

    def grouped(ref, b, r):
        parts = [ref[b, pl.ds(r, 1), g * HEAD_SIZE : (g + 1) * HEAD_SIZE] for g in range(kv_heads)]
        return jnp.concatenate(
            [jnp.broadcast_to(part, (group, HEAD_SIZE)) for part in parts], axis=0
        )

    def stacked(ref, b, r):
        return jnp.concatenate(
            [ref[b, r, :, g * HEAD_SIZE : (g + 1) * HEAD_SIZE] for g in range(kv_heads)], axis=0
        )

    def attend(b, r):
        picked = pl.ds(r, heads, stride=rows)
        q = q_rows[b, picked, :]
        score = lax.dot_general(
            q.astype(jnp.bfloat16),
            stacked(keys, b, r),
            (((1,), (1,)), ((), ())),
            preferred_element_type=jnp.float32,
        )
        score = jnp.where(position < lengths_ref[b, r], score * scale, -jnp.inf)
        own_score = jnp.sum(q * grouped(own_keys, b, r), axis=1, keepdims=True) * scale
        top = jnp.maximum(jnp.max(score, axis=1, keepdims=True), own_score)
        raised = jnp.exp(score - top)
        own_raised = jnp.exp(own_score - top)
        total = jnp.sum(raised, axis=1, keepdims=True) + own_raised
        probs = (raised / total).astype(jnp.bfloat16)
        own_prob = (own_raised / total).astype(jnp.bfloat16).astype(jnp.float32)
        out = jnp.dot(probs, stacked(values, b, r), preferred_element_type=jnp.float32)
        o_rows[b, picked, :] = out + own_prob * grouped(own_values, b, r)

    def attend_two(b, i):
        attend(b, 2 * i)
        attend(b, 2 * i + 1)

    pairs = [(b, i) for b in range(batches) for i in range(rows // 2)]
    forwards = [("z", step) for step in order] + [("x", step) for step in [0] + order]
    share = -(-len(pairs) // (len(forwards) + 1))

    def attend_share(turn):
        for b, i in pairs[turn * share : (turn + 1) * share]:
            attend_two(b, i)

    attend_share(0)
    for turn, (kind, step) in enumerate(forwards):
        if kind == "z":
            gather_z(step).wait_recv()
            gather_x(step).start()
            gather_c(0, step).start()
        else:
            gather_x(step).wait_recv()
            gather_c(1, step).start()
        attend_share(turn + 1)

    expert = me // PAIR

    def hidden_units(far_core):
        span = pl.ds(far_core * half, half)
        x = gathered[span, 0:width]
        gate_val = jnp.dot(x, w_gate[0], preferred_element_type=jnp.float32)
        up_val = jnp.dot(x, w_up[0], preferred_element_type=jnp.float32)
        act[span, :] = (gate_val / (1.0 + jnp.exp(-gate_val)) * up_val).astype(jnp.bfloat16)
        tail = gathered[span, width:].astype(jnp.float32)
        at = lax.broadcasted_iota(jnp.int32, tail.shape, 1)
        mine = jnp.sum(jnp.where(lax.rem(at, experts) == expert, tail, 0.0), axis=1, keepdims=True)
        row_weight[span, :] = jnp.broadcast_to(mine, (half, LANES))

    loads[2].wait()
    loads[3].wait()
    hidden_units(0)
    for far_side in range(PAIR):
        for step in range(ring):
            gather_c(far_side, step).wait_recv()
    hidden_units(1)
    loads[4].wait()

    def reduce_c(j):
        return remote(send_c.at[j], recv_c.at[j], rc_send.at[j], rc_recv.at[j], mate)

    def reduce_x(j):
        return remote(send_x.at[j], recv_x.at[j], rx_send.at[j], rx_recv.at[j], side)

    def reduce_z(j, step):
        at = j * ring + step
        return remote(
            send_z.at[j, step], recv_z.at[j, step], rz_send.at[at], rz_recv.at[at], down_by(step)
        )

    def project(j):
        columns = slice(j * chunk, (j + 1) * chunk)
        for far_core in (1, 0):
            span = pl.ds(far_core * half, half)
            out = jnp.dot(act[span, :], w_down[0, :, columns], preferred_element_type=jnp.float32)
            out = out * jnp.concatenate([row_weight[span, :]] * (chunk // LANES), axis=1)
            if far_core:
                send_c[j] = out.astype(jnp.bfloat16)
                reduce_c(j).start()
            else:
                keep_c[j] = out

    def after_c(j):
        reduce_c(j).wait_recv()
        for far_side in (1, 0):
            span = slice(far_side * quarter, (far_side + 1) * quarter)
            out = keep_c[j, span, :] + recv_c[j, span, :].astype(jnp.float32)
            if far_side:
                send_x[j] = out.astype(jnp.bfloat16)
                reduce_x(j).start()
            else:
                keep_x[j] = out

    def after_x(j):
        reduce_x(j).wait_recv()
        for step in order + [0]:
            span = slice(step * block, (step + 1) * block)
            out = keep_x[j, span, :] + recv_x[j, span, :].astype(jnp.float32)
            if step:
                send_z[j, step] = out.astype(jnp.bfloat16)
                reduce_z(j, step).start()
            else:
                keep_x[j, span, :] = out

    def after_z(j):
        out = keep_x[j, 0:block, :]
        for step in order:
            reduce_z(j, step).wait_recv()
            out = out + recv_z[j, step].astype(jnp.float32)
        out = out.astype(jnp.bfloat16).astype(jnp.float32)
        for b in range(batches):
            moe_ref[b, :, j * chunk : (j + 1) * chunk] = out[b * rows : (b + 1) * rows].astype(
                jnp.bfloat16
            )

    stages = (project, after_c, after_x, after_z)
    lags = (0, 1, 2, 4)
    for tick in range(chunks + lags[-1]):
        for stage, lag in zip(stages, lags):
            if 0 <= tick - lag < chunks:
                stage(tick - lag)

    for b in range(batches):
        for h in range(heads):
            attn_ref[b, :, h * HEAD_SIZE : (h + 1) * HEAD_SIZE] = o_rows[
                b, h * rows : (h + 1) * rows, :
            ].astype(jnp.bfloat16)

    for step in order:
        gather_z(step).wait_send()
    for step in range(ring):
        gather_x(step).wait_send()
        for far_side in range(PAIR):
            gather_c(far_side, step).wait_send()
    for j in range(chunks):
        reduce_c(j).wait_send()
        reduce_x(j).wait_send()
        for step in order:
            reduce_z(j, step).wait_send()


def dense_shards(
    hidden_in,
    routes,
    gates,
    query,
    cached_key_rows,
    cached_value_rows,
    fresh_key,
    fresh_value,
    lengths,
    w_gate,
    w_up,
    w_down,
):
    ep_size = lax.axis_size("ep")
    experts = ep_size // PAIR
    ring = ep_size // (PAIR * PAIR)
    batches, rows, width = hidden_in.shape
    slots = cached_key_rows.shape[2]
    kv_heads = cached_key_rows.shape[3] // HEAD_SIZE
    heads = query.shape[2] // HEAD_SIZE
    depth = w_gate.shape[2]
    chunks = 4
    chunk = width // chunks
    block = batches * rows
    quarter = ring * block
    half = PAIR * quarter
    spread = -(-2 * experts // LANES) * LANES
    dims = (batches, rows, width, heads, kv_heads, slots, experts, depth, chunks, chunk)
    vmem = pl.BlockSpec(memory_space=pltpu.VMEM)
    smem = pl.BlockSpec(memory_space=pltpu.SMEM)
    anywhere = pl.BlockSpec(memory_space=pl.ANY)
    bf16, f32 = jnp.bfloat16, jnp.float32
    dma = pltpu.SemaphoreType.DMA
    return pl.pallas_call(
        functools.partial(layer_kernel, dims),
        out_shape=(
            jax.ShapeDtypeStruct(query.shape, bf16),
            jax.ShapeDtypeStruct(hidden_in.shape, bf16),
        ),
        in_specs=[vmem] * 6 + [smem] + [anywhere] * 5,
        out_specs=(vmem, vmem),
        scratch_shapes=[
            pltpu.VMEM(cached_key_rows.shape, bf16),
            pltpu.VMEM(cached_value_rows.shape, bf16),
            pltpu.VMEM(w_gate.shape, bf16),
            pltpu.VMEM(w_up.shape, bf16),
            pltpu.VMEM(w_down.shape, bf16),
            pltpu.VMEM((PAIR * half, width + spread), bf16),
            pltpu.VMEM((batches, heads * rows, HEAD_SIZE), f32),
            pltpu.VMEM((batches, heads * rows, HEAD_SIZE), f32),
            pltpu.VMEM(fresh_key.shape, f32),
            pltpu.VMEM(fresh_value.shape, f32),
            pltpu.VMEM((PAIR * half, LANES), f32),
            pltpu.VMEM((PAIR * half, depth), bf16),
            pltpu.VMEM((chunks, half, chunk), f32),
            pltpu.VMEM((chunks, quarter, chunk), f32),
            pltpu.VMEM((chunks, half, chunk), bf16),
            pltpu.VMEM((chunks, half, chunk), bf16),
            pltpu.VMEM((chunks, quarter, chunk), bf16),
            pltpu.VMEM((chunks, quarter, chunk), bf16),
            pltpu.VMEM((chunks, ring, block, chunk), bf16),
            pltpu.VMEM((chunks, ring, block, chunk), bf16),
            dma((5,)),
            dma((ring,)),
            dma((ring,)),
            dma((ring,)),
            dma((ring,)),
            dma((PAIR * ring,)),
            dma((PAIR * ring,)),
            dma((chunks,)),
            dma((chunks,)),
            dma((chunks,)),
            dma((chunks,)),
            dma((chunks * ring,)),
            dma((chunks * ring,)),
        ],
        compiler_params=pltpu.CompilerParams(
            collective_id=0, has_side_effects=True, vmem_limit_bytes=40 * 1024 * 1024
        ),
        cost_estimate=pl.CostEstimate(
            flops=6 * PAIR * half * width * depth, bytes_accessed=8 * 1024 * 1024, transcendentals=0
        ),
    )(
        hidden_in,
        routes,
        gates,
        query,
        fresh_key,
        fresh_value,
        lengths,
        cached_key_rows,
        cached_value_rows,
        w_gate,
        w_up,
        w_down,
    )


def shards(*args):
    hidden_in, routes = args[0], args[1]
    ep_size = lax.axis_size("ep")
    batches, rows, width = hidden_in.shape
    every_expert = routes.shape[2] == ep_size // PAIR
    fits = ep_size % (PAIR * PAIR) == 0 and ep_size > PAIR * PAIR and lax.axis_size("tp") == 1
    tiles = batches * rows % TILE_ROWS == 0 and rows % 8 == 0 and width % (4 * LANES) == 0
    if every_expert and fits and tiles:
        return dense_shards(*args)
    return sparse_shards(*args)


def solution(mesh):
    in_specs = (
        P(None, ("grp", "ep"), None),
        P(None, ("grp", "ep"), None),
        P(None, ("grp", "ep"), None),
        P(None, ("grp", "ep"), "tp"),
        P(None, ("grp", "ep"), None, "tp"),
        P(None, ("grp", "ep"), None, "tp"),
        P(None, ("grp", "ep"), "tp"),
        P(None, ("grp", "ep"), "tp"),
        P(None, ("grp", "ep")),
        P("ep", None, "tp"),
        P("ep", None, "tp"),
        P("ep", "tp", None),
    )
    out_specs = (P(None, ("grp", "ep"), "tp"), P(None, ("grp", "ep"), "tp"))
    return jax.shard_map(shards, mesh=mesh, in_specs=in_specs, out_specs=out_specs, check_vma=False)
```

```python
import functools
import math

import jax
import jax.numpy as jnp
from jax import lax
from jax.experimental import pallas as pl
from jax.experimental.pallas import tpu as pltpu
from jax.sharding import PartitionSpec as P

QUERY_HEADS = 64
KEY_VALUE_HEADS = 4
HEAD_SIZE = 128


def swapped(block, axis, bit):
    count = lax.axis_size(axis)
    route = []
    for low in range(count):
        high = low | 1 << bit
        if high != low and high < count:
            route += [(low, high), (high, low)]
    return lax.ppermute(block, axis, route)


def attend_local(query_rows, cached_key_rows, cached_value_rows, fresh_key, fresh_value, lengths):
    row_count = query_rows.shape[0]
    query_group = QUERY_HEADS // KEY_VALUE_HEADS
    kv_local = cached_key_rows.shape[2] // HEAD_SIZE
    cache_len = cached_key_rows.shape[1]
    grouped_query_rows = query_rows.reshape(row_count, kv_local, query_group, HEAD_SIZE)
    earlier_keys = cached_key_rows.reshape(row_count, cache_len, kv_local, HEAD_SIZE)
    earlier_values = cached_value_rows.reshape(row_count, cache_len, kv_local, HEAD_SIZE)
    token_own_keys = fresh_key.reshape(row_count, kv_local, HEAD_SIZE)
    token_own_values = fresh_value.reshape(row_count, kv_local, HEAD_SIZE).astype(jnp.float32)
    score_scale = 1.0 / math.sqrt(HEAD_SIZE)
    past_score = (
        jnp.einsum(
            "rkgd,rckd->rkgc", grouped_query_rows, earlier_keys, preferred_element_type=jnp.float32
        )
        * score_scale
    )
    own_score = (
        jnp.einsum(
            "rkgd,rkd->rkg", grouped_query_rows, token_own_keys, preferred_element_type=jnp.float32
        )[..., None]
        * score_scale
    )
    valid_pos = lax.broadcasted_iota(jnp.int32, (row_count, cache_len), 1) < lengths[:, None]
    past_score = jnp.where(valid_pos[:, None, None, :], past_score, -jnp.inf)
    scores = jnp.concatenate([past_score, own_score], axis=-1)
    row_max = jnp.max(scores, axis=-1, keepdims=True)
    exp_scores = jnp.exp(scores - row_max)
    weights_bf = (exp_scores / jnp.sum(exp_scores, axis=-1, keepdims=True)).astype(jnp.bfloat16)
    attended = jnp.einsum(
        "rkgc,rckd->rkgd",
        weights_bf[..., :cache_len],
        earlier_values,
        preferred_element_type=jnp.float32,
    )
    attended = (
        attended + weights_bf[..., cache_len:].astype(jnp.float32) * token_own_values[:, :, None, :]
    )
    return attended.reshape(row_count, kv_local * query_group * HEAD_SIZE).astype(jnp.bfloat16)


def slot_layout(route_rows, experts, capacity):
    flat_routes = route_rows.reshape(-1)
    onehot = (flat_routes[:, None] == jnp.arange(experts, dtype=jnp.int32)[None, :]).astype(
        jnp.int32
    )
    before = jnp.cumsum(onehot, axis=0) - onehot
    slot_rank = jnp.sum(before * onehot, axis=1)
    return 2 * flat_routes * capacity + slot_rank


def pack_rows(tokens, first_slot, capacity, slot_total, route_count):
    targets = jnp.stack([first_slot, first_slot + capacity], axis=1)
    slot_ids = lax.broadcasted_iota(jnp.int32, (slot_total, 1, 1), 0)
    chosen = jnp.sum((targets[None, :, :] == slot_ids).astype(jnp.float32), axis=2)
    chosen = jnp.sum(chosen.reshape(slot_total, -1, route_count), axis=2).astype(jnp.bfloat16)
    return jnp.dot(chosen, tokens, preferred_element_type=jnp.float32).astype(jnp.bfloat16)


def combine_rows(returned, first_slot, capacity, row_gates, row_count, route_count):
    flat_back = returned.reshape(returned.shape[0] * returned.shape[1], returned.shape[2])
    lower = jnp.take(flat_back, first_slot, axis=0)
    upper = jnp.take(flat_back, first_slot + capacity, axis=0)
    outputs = jnp.concatenate([lower, upper], axis=1)
    outputs = lax.optimization_barrier(outputs).astype(jnp.float32)
    weighted = row_gates.reshape(-1, 1) * outputs
    return jnp.sum(weighted.reshape(row_count, route_count, -1), axis=1).astype(jnp.bfloat16)


def sparse_shards(
    hidden_in,
    routes,
    gates,
    query,
    cached_key_rows,
    cached_value_rows,
    fresh_key,
    fresh_value,
    lengths,
    w_gate,
    w_up,
    w_down,
):
    ep_size = lax.axis_size("ep")
    experts = ep_size // 2
    batches, row_count, route_count = routes.shape
    model_width = hidden_in.shape[2]
    capacity = min(row_count, 2 * ((row_count * route_count + experts - 1) // experts))
    slot_total = ep_size * capacity
    layouts = []
    buffers = []
    for batch_idx in range(batches):
        first_slot = slot_layout(routes[batch_idx], experts, capacity)
        layouts.append(first_slot)
        packed = pack_rows(hidden_in[batch_idx], first_slot, capacity, slot_total, route_count)
        buffers.append(packed.reshape(ep_size, capacity, model_width))
    attn_list = []
    blocks = []
    for batch_idx in range(batches):
        received = lax.all_to_all(buffers[batch_idx], "ep", split_axis=0, concat_axis=0, tiled=True)
        item_count = received.shape[1]
        slot_rows = received.reshape(ep_size * item_count, model_width)
        gate_val = jnp.dot(slot_rows, w_gate[0], preferred_element_type=jnp.float32)
        up_val = jnp.dot(slot_rows, w_up[0], preferred_element_type=jnp.float32)
        hidden = (jax.nn.silu(gate_val) * up_val).astype(jnp.bfloat16)
        partial_value = jnp.dot(hidden, w_down[0], preferred_element_type=jnp.float32)
        partial_value = partial_value.reshape(ep_size, item_count, model_width)
        half_sum = lax.psum_scatter(partial_value, "tp", scatter_dimension=2, tiled=True)
        partner = swapped(half_sum, "ep", 0)
        finished = (half_sum + partner).astype(jnp.bfloat16)
        quarter = finished.shape[2] // 2
        parity = lax.axis_index("ep") % 2
        quarter_cols = lax.dynamic_slice_in_dim(finished, parity * quarter, quarter, 2)
        blocks.append(lax.all_to_all(quarter_cols, "ep", split_axis=0, concat_axis=0, tiled=True))
        attn_list.append(
            attend_local(
                query[batch_idx],
                cached_key_rows[batch_idx],
                cached_value_rows[batch_idx],
                fresh_key[batch_idx],
                fresh_value[batch_idx],
                lengths[batch_idx],
            )
        )
    moe_list = []
    for batch_idx in range(batches):
        moe_list.append(
            combine_rows(
                blocks[batch_idx],
                layouts[batch_idx],
                capacity,
                gates[batch_idx],
                row_count,
                route_count,
            )
        )
    return (jnp.stack(attn_list), jnp.stack(moe_list))


LANES = 128
TILE_ROWS = 16
PAIR = 2
MESH = pl.DeviceIdType.MESH


def remote(src, dst, send_sem, recv_sem, index):
    return pltpu.make_async_remote_copy(
        src_ref=src,
        dst_ref=dst,
        send_sem=send_sem,
        recv_sem=recv_sem,
        device_id={"ep": index},
        device_id_type=MESH,
    )


def layer_kernel(
    dims,
    lengths_ref,
    hidden_hbm,
    routes_hbm,
    gates_hbm,
    query_hbm,
    fresh_key_hbm,
    fresh_value_hbm,
    key_hbm,
    value_hbm,
    gate_hbm,
    up_hbm,
    down_hbm,
    attn_ref,
    moe_ref,
    hidden_ref,
    routes_ref,
    gates_ref,
    query_ref,
    fresh_key_ref,
    fresh_value_ref,
    keys,
    values,
    w_gate,
    w_up,
    w_down,
    gathered,
    q_rows,
    o_rows,
    own_keys,
    own_values,
    row_weight,
    act,
    keep_c,
    keep_x,
    send_c,
    recv_c,
    send_x,
    recv_x,
    send_z,
    recv_z,
    load_sems,
    gz_send,
    gz_recv,
    gx_send,
    gx_recv,
    gc_send,
    gc_recv,
    rc_send,
    rc_recv,
    rx_send,
    rx_recv,
    rz_send,
    rz_recv,
):
    batches, rows, width, heads, kv_heads, slots, experts, depth, chunks, chunk = dims
    ring = gz_send.shape[0]
    block = batches * rows
    quarter = ring * block
    half = PAIR * quarter
    group = heads // kv_heads
    scale = 1.0 / math.sqrt(HEAD_SIZE)

    me = lax.axis_index("ep")
    core = lax.rem(me, PAIR)
    across = lax.rem(me // PAIR, PAIR)
    place = lax.rem(me, PAIR * PAIR)
    level = me // (PAIR * PAIR)
    mate = me + 1 - PAIR * core
    side = me + PAIR - PAIR * PAIR * across

    def up_by(step):
        return lax.rem(level + step, ring) * (PAIR * PAIR) + place

    def down_by(step):
        return lax.rem(level + ring - step, ring) * (PAIR * PAIR) + place

    loads = [
        pltpu.make_async_copy(source, target, load_sems.at[i])
        for i, (source, target) in enumerate(
            (
                (hidden_hbm, hidden_ref),
                (routes_hbm, routes_ref),
                (gates_hbm, gates_ref),
                (query_hbm, query_ref),
                (fresh_key_hbm, fresh_key_ref),
                (fresh_value_hbm, fresh_value_ref),
                (key_hbm, keys),
                (value_hbm, values),
                (gate_hbm, w_gate),
                (up_hbm, w_up),
                (down_hbm, w_down),
            )
        )
    ]
    for load in loads:
        load.start()

    barrier = pltpu.get_barrier_semaphore()
    others = [mate, side] + [up_by(step) for step in range(1, ring)]
    for other in others:
        pl.semaphore_signal(barrier, inc=1, device_id={"ep": other}, device_id_type=MESH)

    for load in loads[0:3]:
        load.wait()
    gathered[0:block, 0:width] = hidden_ref[...]
    spread = gathered.shape[1] - width
    lane = lax.broadcasted_iota(jnp.int32, (rows, spread), 1)
    expert_of = lax.rem(lane, experts)
    tails = []
    for b in range(batches):
        dense = jnp.zeros((rows, spread), jnp.float32)
        for k in range(routes_ref.shape[2]):
            named = routes_ref[b, :, k : k + 1] == expert_of
            dense = dense + jnp.where(named, gates_ref[b, :, k : k + 1], 0.0)
        high = dense.astype(jnp.bfloat16).astype(jnp.float32)
        tail = jnp.where(lane < experts, high, dense - high)
        tails.append(jnp.where(lane < 2 * experts, tail, 0.0))
    gathered[0:block, width:] = jnp.concatenate(tails, axis=0).astype(jnp.bfloat16)

    pl.semaphore_wait(barrier, len(others))

    def slot(far_core, far_side, step):
        return pl.ds(((far_core * PAIR + far_side) * ring + step) * block, block)

    def gather_z(step):
        return remote(
            gathered.at[slot(0, 0, 0)],
            gathered.at[slot(0, 0, step)],
            gz_send.at[step],
            gz_recv.at[step],
            up_by(step),
        )

    def gather_x(step):
        return remote(
            gathered.at[slot(0, 0, step)],
            gathered.at[slot(0, 1, step)],
            gx_send.at[step],
            gx_recv.at[step],
            side,
        )

    def gather_c(far_side, step):
        return remote(
            gathered.at[slot(0, far_side, step)],
            gathered.at[slot(1, far_side, step)],
            gc_send.at[far_side * ring + step],
            gc_recv.at[far_side * ring + step],
            mate,
        )

    order = sorted(range(1, ring), key=lambda step: min(step, ring - step))
    for step in order:
        gather_z(step).start()
    gather_x(0).start()
    gather_c(0, 0).start()

    for load in loads[3:8]:
        load.wait()
    own_keys[...] = fresh_key_ref[...].astype(jnp.float32)
    own_values[...] = fresh_value_ref[...].astype(jnp.float32)
    for h in range(heads):
        q_rows[h * block : (h + 1) * block, :] = query_ref[
            :, h * HEAD_SIZE : (h + 1) * HEAD_SIZE
        ].astype(jnp.float32)

    head = lax.broadcasted_iota(jnp.int32, (heads, kv_heads * slots), 0)
    column = lax.broadcasted_iota(jnp.int32, (heads, kv_heads * slots), 1)
    position = jnp.where(head // group == column // slots, lax.rem(column, slots), slots)

    def grouped(ref, row):
        parts = [ref[row : row + 1, g * HEAD_SIZE : (g + 1) * HEAD_SIZE] for g in range(kv_heads)]
        return jnp.concatenate(
            [jnp.broadcast_to(part, (group, HEAD_SIZE)) for part in parts], axis=0
        )

    def stacked(ref, b, r):
        return jnp.concatenate(
            [ref[b, r, :, g * HEAD_SIZE : (g + 1) * HEAD_SIZE] for g in range(kv_heads)], axis=0
        )

    def attend(row):
        b, r = divmod(row, rows)
        picked = pl.ds(row, heads, stride=block)
        q = q_rows[picked, :]
        score = lax.dot_general(
            q.astype(jnp.bfloat16),
            stacked(keys, b, r),
            (((1,), (1,)), ((), ())),
            preferred_element_type=jnp.float32,
        )
        score = jnp.where(position < lengths_ref[b, r], score * scale, -jnp.inf)
        own_score = jnp.sum(q * grouped(own_keys, row), axis=1, keepdims=True) * scale
        top = jnp.maximum(jnp.max(score, axis=1, keepdims=True), own_score)
        raised = jnp.exp(score - top)
        own_raised = jnp.exp(own_score - top)
        share = 1.0 / (jnp.sum(raised, axis=1, keepdims=True) + own_raised)
        probs = (raised * share).astype(jnp.bfloat16)
        own_prob = (own_raised * share).astype(jnp.bfloat16).astype(jnp.float32)
        out = jnp.dot(probs, stacked(values, b, r), preferred_element_type=jnp.float32)
        o_rows[picked, :] = out + own_prob * grouped(own_values, row)

    todo = list(range(block))

    def attend_some(count):
        for _ in range(min(count, len(todo))):
            attend(todo.pop(0))

    attend_some(2)
    for step in order:
        gather_z(step).wait_recv()
        gather_x(step).start()
        gather_c(0, step).start()
        attend_some(1)
    for step in [0] + order:
        gather_x(step).wait_recv()
        gather_c(1, step).start()
        attend_some(1)

    expert = me // PAIR

    def hidden_units(far_core):
        span = pl.ds(far_core * half, half)
        x = gathered[span, 0:width]
        gate_val = jnp.dot(x, w_gate[0], preferred_element_type=jnp.float32)
        up_val = jnp.dot(x, w_up[0], preferred_element_type=jnp.float32)
        act[span, :] = (gate_val / (1.0 + jnp.exp(-gate_val)) * up_val).astype(jnp.bfloat16)
        tail = gathered[span, width:].astype(jnp.float32)
        at = lax.broadcasted_iota(jnp.int32, tail.shape, 1)
        mine = jnp.sum(jnp.where(lax.rem(at, experts) == expert, tail, 0.0), axis=1, keepdims=True)
        row_weight[span, :] = jnp.broadcast_to(mine, (half, LANES))

    loads[8].wait()
    loads[9].wait()
    hidden_units(0)
    for far_side in range(PAIR):
        for step in range(ring):
            gather_c(far_side, step).wait_recv()
    hidden_units(1)
    loads[10].wait()

    def reduce_c(j):
        return remote(send_c.at[j], recv_c.at[j], rc_send.at[j], rc_recv.at[j], mate)

    def reduce_x(j):
        return remote(send_x.at[j], recv_x.at[j], rx_send.at[j], rx_recv.at[j], side)

    def reduce_z(j, step):
        at = j * ring + step
        return remote(
            send_z.at[j, step], recv_z.at[j, step], rz_send.at[at], rz_recv.at[at], down_by(step)
        )

    def project(j):
        columns = slice(j * chunk, (j + 1) * chunk)
        for far_core in (1, 0):
            span = pl.ds(far_core * half, half)
            out = jnp.dot(act[span, :], w_down[0, :, columns], preferred_element_type=jnp.float32)
            out = out * jnp.concatenate([row_weight[span, :]] * (chunk // LANES), axis=1)
            if far_core:
                send_c[j] = out.astype(jnp.bfloat16)
                reduce_c(j).start()
            else:
                keep_c[j] = out

    def after_c(j):
        reduce_c(j).wait_recv()
        for far_side in (1, 0):
            span = slice(far_side * quarter, (far_side + 1) * quarter)
            out = keep_c[j, span, :] + recv_c[j, span, :].astype(jnp.float32)
            if far_side:
                send_x[j] = out.astype(jnp.bfloat16)
                reduce_x(j).start()
            else:
                keep_x[j] = out

    def after_x(j):
        reduce_x(j).wait_recv()
        for step in order + [0]:
            span = slice(step * block, (step + 1) * block)
            out = keep_x[j, span, :] + recv_x[j, span, :].astype(jnp.float32)
            if step:
                send_z[j, step] = out.astype(jnp.bfloat16)
                reduce_z(j, step).start()
            else:
                keep_x[j, span, :] = out

    def after_z(j):
        out = keep_x[j, 0:block, :]
        for step in order:
            reduce_z(j, step).wait_recv()
            out = out + recv_z[j, step].astype(jnp.float32)
        moe_ref[:, j * chunk : (j + 1) * chunk] = out.astype(jnp.bfloat16)

    for tick in range(chunks + 2):
        if tick < chunks:
            project(tick)
        if tick >= 2:
            after_c(tick - 2)
    attend_some(2)
    for j in range(chunks):
        after_x(j)
        attend_some(1)
    attend_some(block)
    for h in range(heads):
        attn_ref[:, h * HEAD_SIZE : (h + 1) * HEAD_SIZE] = o_rows[
            h * block : (h + 1) * block, :
        ].astype(jnp.bfloat16)
    for j in range(chunks):
        after_z(j)

    for step in order:
        gather_z(step).wait_send()
    for step in range(ring):
        gather_x(step).wait_send()
        for far_side in range(PAIR):
            gather_c(far_side, step).wait_send()
    for j in range(chunks):
        reduce_c(j).wait_send()
        reduce_x(j).wait_send()
        for step in order:
            reduce_z(j, step).wait_send()


def dense_shards(
    hidden_in,
    routes,
    gates,
    query,
    cached_key_rows,
    cached_value_rows,
    fresh_key,
    fresh_value,
    lengths,
    w_gate,
    w_up,
    w_down,
):
    ep_size = lax.axis_size("ep")
    experts = ep_size // PAIR
    ring = ep_size // (PAIR * PAIR)
    batches, rows, width = hidden_in.shape
    slots = cached_key_rows.shape[2]
    kv_heads = cached_key_rows.shape[3] // HEAD_SIZE
    heads = query.shape[2] // HEAD_SIZE
    depth = w_gate.shape[2]
    chunks = 8
    chunk = width // chunks
    block = batches * rows
    quarter = ring * block
    half = PAIR * quarter
    spread = -(-2 * experts // LANES) * LANES
    dims = (batches, rows, width, heads, kv_heads, slots, experts, depth, chunks, chunk)
    vmem = pl.BlockSpec(memory_space=pltpu.VMEM)
    smem = pl.BlockSpec(memory_space=pltpu.SMEM)
    anywhere = pl.BlockSpec(memory_space=pl.ANY)
    bf16, f32 = jnp.bfloat16, jnp.float32
    dma = pltpu.SemaphoreType.DMA
    def flat(array):
        return array.reshape(block, array.shape[2])

    attn_out, moe_out = pl.pallas_call(
        functools.partial(layer_kernel, dims),
        out_shape=(
            jax.ShapeDtypeStruct((block, query.shape[2]), bf16),
            jax.ShapeDtypeStruct((block, width), bf16),
        ),
        in_specs=[smem] + [anywhere] * 11,
        out_specs=(vmem, vmem),
        scratch_shapes=[
            pltpu.VMEM((block, width), bf16),
            pltpu.VMEM(routes.shape, jnp.int32),
            pltpu.VMEM(gates.shape, f32),
            pltpu.VMEM((block, query.shape[2]), bf16),
            pltpu.VMEM((block, fresh_key.shape[2]), bf16),
            pltpu.VMEM((block, fresh_value.shape[2]), bf16),
            pltpu.VMEM(cached_key_rows.shape, bf16),
            pltpu.VMEM(cached_value_rows.shape, bf16),
            pltpu.VMEM(w_gate.shape, bf16),
            pltpu.VMEM(w_up.shape, bf16),
            pltpu.VMEM(w_down.shape, bf16),
            pltpu.VMEM((PAIR * half, width + spread), bf16),
            pltpu.VMEM((heads * block, HEAD_SIZE), f32),
            pltpu.VMEM((heads * block, HEAD_SIZE), f32),
            pltpu.VMEM((block, fresh_key.shape[2]), f32),
            pltpu.VMEM((block, fresh_value.shape[2]), f32),
            pltpu.VMEM((PAIR * half, LANES), f32),
            pltpu.VMEM((PAIR * half, depth), bf16),
            pltpu.VMEM((chunks, half, chunk), f32),
            pltpu.VMEM((chunks, quarter, chunk), f32),
            pltpu.VMEM((chunks, half, chunk), bf16),
            pltpu.VMEM((chunks, half, chunk), bf16),
            pltpu.VMEM((chunks, quarter, chunk), bf16),
            pltpu.VMEM((chunks, quarter, chunk), bf16),
            pltpu.VMEM((chunks, ring, block, chunk), bf16),
            pltpu.VMEM((chunks, ring, block, chunk), bf16),
            dma((11,)),
            dma((ring,)),
            dma((ring,)),
            dma((ring,)),
            dma((ring,)),
            dma((PAIR * ring,)),
            dma((PAIR * ring,)),
            dma((chunks,)),
            dma((chunks,)),
            dma((chunks,)),
            dma((chunks,)),
            dma((chunks * ring,)),
            dma((chunks * ring,)),
        ],
        compiler_params=pltpu.CompilerParams(
            collective_id=0, has_side_effects=True, vmem_limit_bytes=63 * 1024 * 1024
        ),
        cost_estimate=pl.CostEstimate(
            flops=6 * PAIR * half * width * depth, bytes_accessed=8 * 1024 * 1024, transcendentals=0
        ),
    )(
        lengths,
        flat(hidden_in),
        routes,
        gates,
        flat(query),
        flat(fresh_key),
        flat(fresh_value),
        cached_key_rows,
        cached_value_rows,
        w_gate,
        w_up,
        w_down,
    )
    return attn_out.reshape(query.shape), moe_out.reshape(hidden_in.shape)


def shards(*args):
    hidden_in, routes = args[0], args[1]
    ep_size = lax.axis_size("ep")
    batches, rows, width = hidden_in.shape
    every_expert = routes.shape[2] == ep_size // PAIR
    fits = ep_size % (PAIR * PAIR) == 0 and ep_size > PAIR * PAIR and lax.axis_size("tp") == 1
    tiles = batches * rows % TILE_ROWS == 0 and rows % 8 == 0 and width % (8 * LANES) == 0
    if every_expert and fits and tiles:
        return dense_shards(*args)
    return sparse_shards(*args)


def solution(mesh):
    in_specs = (
        P(None, ("grp", "ep"), None),
        P(None, ("grp", "ep"), None),
        P(None, ("grp", "ep"), None),
        P(None, ("grp", "ep"), "tp"),
        P(None, ("grp", "ep"), None, "tp"),
        P(None, ("grp", "ep"), None, "tp"),
        P(None, ("grp", "ep"), "tp"),
        P(None, ("grp", "ep"), "tp"),
        P(None, ("grp", "ep")),
        P("ep", None, "tp"),
        P("ep", None, "tp"),
        P("ep", "tp", None),
    )
    out_specs = (P(None, ("grp", "ep"), "tp"), P(None, ("grp", "ep"), "tp"))
    return jax.shard_map(shards, mesh=mesh, in_specs=in_specs, out_specs=out_specs, check_vma=False)
```

```python
import functools
import math

import jax
import jax.numpy as jnp
from jax import lax
from jax.experimental import pallas as pl
from jax.experimental.pallas import tpu as pltpu
from jax.sharding import PartitionSpec as P

QUERY_HEADS = 64
KEY_VALUE_HEADS = 4
HEAD_SIZE = 128


def swapped(block, axis, bit):
    count = lax.axis_size(axis)
    route = []
    for low in range(count):
        high = low | 1 << bit
        if high != low and high < count:
            route += [(low, high), (high, low)]
    return lax.ppermute(block, axis, route)


def attend_local(query_rows, cached_key_rows, cached_value_rows, fresh_key, fresh_value, lengths):
    row_count = query_rows.shape[0]
    query_group = QUERY_HEADS // KEY_VALUE_HEADS
    kv_local = cached_key_rows.shape[2] // HEAD_SIZE
    cache_len = cached_key_rows.shape[1]
    grouped_query_rows = query_rows.reshape(row_count, kv_local, query_group, HEAD_SIZE)
    earlier_keys = cached_key_rows.reshape(row_count, cache_len, kv_local, HEAD_SIZE)
    earlier_values = cached_value_rows.reshape(row_count, cache_len, kv_local, HEAD_SIZE)
    token_own_keys = fresh_key.reshape(row_count, kv_local, HEAD_SIZE)
    token_own_values = fresh_value.reshape(row_count, kv_local, HEAD_SIZE).astype(jnp.float32)
    score_scale = 1.0 / math.sqrt(HEAD_SIZE)
    past_score = (
        jnp.einsum(
            "rkgd,rckd->rkgc", grouped_query_rows, earlier_keys, preferred_element_type=jnp.float32
        )
        * score_scale
    )
    own_score = (
        jnp.einsum(
            "rkgd,rkd->rkg", grouped_query_rows, token_own_keys, preferred_element_type=jnp.float32
        )[..., None]
        * score_scale
    )
    valid_pos = lax.broadcasted_iota(jnp.int32, (row_count, cache_len), 1) < lengths[:, None]
    past_score = jnp.where(valid_pos[:, None, None, :], past_score, -jnp.inf)
    scores = jnp.concatenate([past_score, own_score], axis=-1)
    row_max = jnp.max(scores, axis=-1, keepdims=True)
    exp_scores = jnp.exp(scores - row_max)
    weights_bf = (exp_scores / jnp.sum(exp_scores, axis=-1, keepdims=True)).astype(jnp.bfloat16)
    attended = jnp.einsum(
        "rkgc,rckd->rkgd",
        weights_bf[..., :cache_len],
        earlier_values,
        preferred_element_type=jnp.float32,
    )
    attended = (
        attended + weights_bf[..., cache_len:].astype(jnp.float32) * token_own_values[:, :, None, :]
    )
    return attended.reshape(row_count, kv_local * query_group * HEAD_SIZE).astype(jnp.bfloat16)


def slot_layout(route_rows, experts, capacity):
    flat_routes = route_rows.reshape(-1)
    onehot = (flat_routes[:, None] == jnp.arange(experts, dtype=jnp.int32)[None, :]).astype(
        jnp.int32
    )
    before = jnp.cumsum(onehot, axis=0) - onehot
    slot_rank = jnp.sum(before * onehot, axis=1)
    return 2 * flat_routes * capacity + slot_rank


def pack_rows(tokens, first_slot, capacity, slot_total, route_count):
    targets = jnp.stack([first_slot, first_slot + capacity], axis=1)
    slot_ids = lax.broadcasted_iota(jnp.int32, (slot_total, 1, 1), 0)
    chosen = jnp.sum((targets[None, :, :] == slot_ids).astype(jnp.float32), axis=2)
    chosen = jnp.sum(chosen.reshape(slot_total, -1, route_count), axis=2).astype(jnp.bfloat16)
    return jnp.dot(chosen, tokens, preferred_element_type=jnp.float32).astype(jnp.bfloat16)


def combine_rows(returned, first_slot, capacity, row_gates, row_count, route_count):
    flat_back = returned.reshape(returned.shape[0] * returned.shape[1], returned.shape[2])
    lower = jnp.take(flat_back, first_slot, axis=0)
    upper = jnp.take(flat_back, first_slot + capacity, axis=0)
    outputs = jnp.concatenate([lower, upper], axis=1)
    outputs = lax.optimization_barrier(outputs).astype(jnp.float32)
    weighted = row_gates.reshape(-1, 1) * outputs
    return jnp.sum(weighted.reshape(row_count, route_count, -1), axis=1).astype(jnp.bfloat16)


def sparse_shards(
    hidden_in,
    routes,
    gates,
    query,
    cached_key_rows,
    cached_value_rows,
    fresh_key,
    fresh_value,
    lengths,
    w_gate,
    w_up,
    w_down,
):
    ep_size = lax.axis_size("ep")
    experts = ep_size // 2
    batches, row_count, route_count = routes.shape
    model_width = hidden_in.shape[2]
    capacity = min(row_count, 2 * ((row_count * route_count + experts - 1) // experts))
    slot_total = ep_size * capacity
    layouts = []
    buffers = []
    for batch_idx in range(batches):
        first_slot = slot_layout(routes[batch_idx], experts, capacity)
        layouts.append(first_slot)
        packed = pack_rows(hidden_in[batch_idx], first_slot, capacity, slot_total, route_count)
        buffers.append(packed.reshape(ep_size, capacity, model_width))
    attn_list = []
    blocks = []
    for batch_idx in range(batches):
        received = lax.all_to_all(buffers[batch_idx], "ep", split_axis=0, concat_axis=0, tiled=True)
        item_count = received.shape[1]
        slot_rows = received.reshape(ep_size * item_count, model_width)
        gate_val = jnp.dot(slot_rows, w_gate[0], preferred_element_type=jnp.float32)
        up_val = jnp.dot(slot_rows, w_up[0], preferred_element_type=jnp.float32)
        hidden = (jax.nn.silu(gate_val) * up_val).astype(jnp.bfloat16)
        partial_value = jnp.dot(hidden, w_down[0], preferred_element_type=jnp.float32)
        partial_value = partial_value.reshape(ep_size, item_count, model_width)
        half_sum = lax.psum_scatter(partial_value, "tp", scatter_dimension=2, tiled=True)
        partner = swapped(half_sum, "ep", 0)
        finished = (half_sum + partner).astype(jnp.bfloat16)
        quarter = finished.shape[2] // 2
        parity = lax.axis_index("ep") % 2
        quarter_cols = lax.dynamic_slice_in_dim(finished, parity * quarter, quarter, 2)
        blocks.append(lax.all_to_all(quarter_cols, "ep", split_axis=0, concat_axis=0, tiled=True))
        attn_list.append(
            attend_local(
                query[batch_idx],
                cached_key_rows[batch_idx],
                cached_value_rows[batch_idx],
                fresh_key[batch_idx],
                fresh_value[batch_idx],
                lengths[batch_idx],
            )
        )
    moe_list = []
    for batch_idx in range(batches):
        moe_list.append(
            combine_rows(
                blocks[batch_idx],
                layouts[batch_idx],
                capacity,
                gates[batch_idx],
                row_count,
                route_count,
            )
        )
    return (jnp.stack(attn_list), jnp.stack(moe_list))


LANES = 128
TILE_ROWS = 16
PAIR = 2
MESH = pl.DeviceIdType.MESH


def remote(src, dst, send_sem, recv_sem, index):
    return pltpu.make_async_remote_copy(
        src_ref=src,
        dst_ref=dst,
        send_sem=send_sem,
        recv_sem=recv_sem,
        device_id={"ep": index},
        device_id_type=MESH,
    )


def layer_kernel(
    dims,
    lengths_ref,
    hidden_hbm,
    routes_hbm,
    gates_hbm,
    query_hbm,
    fresh_key_hbm,
    fresh_value_hbm,
    key_hbm,
    value_hbm,
    gate_hbm,
    up_hbm,
    down_hbm,
    attn_hbm,
    moe_hbm,
    attn_ref,
    moe_ref,
    hidden_ref,
    routes_ref,
    gates_ref,
    query_ref,
    fresh_key_ref,
    fresh_value_ref,
    keys,
    values,
    w_gate,
    w_up,
    w_down,
    gathered,
    q_rows,
    o_rows,
    own_keys,
    own_values,
    row_weight,
    act,
    keep_c,
    keep_x,
    send_c,
    recv_c,
    send_x,
    recv_x,
    send_z,
    recv_z,
    load_sems,
    gz_send,
    gz_recv,
    gx_send,
    gx_recv,
    gc_send,
    gc_recv,
    rc_send,
    rc_recv,
    rx_send,
    rx_recv,
    rz_send,
    rz_recv,
):
    batches, rows, width, heads, kv_heads, slots, experts, depth, chunks, chunk = dims
    ring = gz_send.shape[0]
    block = batches * rows
    quarter = ring * block
    half = PAIR * quarter
    group = heads // kv_heads
    scale = 1.0 / math.sqrt(HEAD_SIZE)

    me = lax.axis_index("ep")
    core = lax.rem(me, PAIR)
    across = lax.rem(me // PAIR, PAIR)
    place = lax.rem(me, PAIR * PAIR)
    level = me // (PAIR * PAIR)
    mate = me + 1 - PAIR * core
    side = me + PAIR - PAIR * PAIR * across

    def up_by(step):
        return lax.rem(level + step, ring) * (PAIR * PAIR) + place

    shorter = jnp.minimum(level, ring - 1 - level)
    longer = 1 - 2 * (level // ((ring + 1) // 2))

    def nearest(turn):
        distance = jnp.where(turn <= 2 * shorter, (turn + 1) // 2, turn - shorter)
        towards = jnp.where(turn <= 2 * shorter, (2 * (turn % 2) - 1) * longer, longer)
        return lax.rem(distance * towards + ring, ring)

    def down_by(step):
        return lax.rem(level + ring - step, ring) * (PAIR * PAIR) + place

    loads = [
        pltpu.make_async_copy(source, target, load_sems.at[i])
        for i, (source, target) in enumerate(
            (
                (hidden_hbm, hidden_ref),
                (routes_hbm, routes_ref),
                (gates_hbm, gates_ref),
                (query_hbm, query_ref),
                (fresh_key_hbm, fresh_key_ref),
                (fresh_value_hbm, fresh_value_ref),
                (key_hbm, keys),
                (value_hbm, values),
                (gate_hbm, w_gate),
                (up_hbm, w_up),
                (down_hbm, w_down),
            )
        )
    ]
    for load in loads:
        load.start()

    barrier = pltpu.get_barrier_semaphore()
    others = [mate, side] + [up_by(step) for step in range(1, ring)]
    for other in others:
        pl.semaphore_signal(barrier, inc=1, device_id={"ep": other}, device_id_type=MESH)

    for load in loads[0:3]:
        load.wait()
    gathered[0:block, 0:width] = hidden_ref[...]
    spread = gathered.shape[1] - width
    lane = lax.broadcasted_iota(jnp.int32, (rows, spread), 1)
    expert_of = lax.rem(lane, experts)
    tails = []
    for b in range(batches):
        dense = jnp.zeros((rows, spread), jnp.float32)
        for k in range(routes_ref.shape[2]):
            named = routes_ref[b, :, k : k + 1] == expert_of
            dense = dense + jnp.where(named, gates_ref[b, :, k : k + 1], 0.0)
        high = dense.astype(jnp.bfloat16).astype(jnp.float32)
        tail = jnp.where(lane < experts, high, dense - high)
        tails.append(jnp.where(lane < 2 * experts, tail, 0.0))
    gathered[0:block, width:] = jnp.concatenate(tails, axis=0).astype(jnp.bfloat16)

    pl.semaphore_wait(barrier, len(others))

    def slot(far_core, far_side, step):
        start = ((far_core * PAIR + far_side) * ring + step) * block
        return pl.ds(pl.multiple_of(start, block), block)

    def gather_z(step):
        return remote(
            gathered.at[slot(0, 0, 0)],
            gathered.at[slot(0, 0, step)],
            gz_send.at[step],
            gz_recv.at[step],
            up_by(step),
        )

    def gather_x(step):
        return remote(
            gathered.at[slot(0, 0, step)],
            gathered.at[slot(0, 1, step)],
            gx_send.at[step],
            gx_recv.at[step],
            side,
        )

    def gather_c(far_side, step):
        return remote(
            gathered.at[slot(0, far_side, step)],
            gathered.at[slot(1, far_side, step)],
            gc_send.at[far_side * ring + step],
            gc_recv.at[far_side * ring + step],
            mate,
        )

    order = list(range(1, ring))
    to_near = [nearest(turn) for turn in order]
    from_near = [lax.rem(ring - step, ring) for step in to_near]
    for step in to_near:
        gather_z(step).start()
    gather_x(0).start()
    gather_c(0, 0).start()

    for load in loads[3:8]:
        load.wait()
    own_keys[...] = fresh_key_ref[...].astype(jnp.float32)
    own_values[...] = fresh_value_ref[...].astype(jnp.float32)
    for h in range(heads):
        q_rows[h * block : (h + 1) * block, :] = query_ref[
            :, h * HEAD_SIZE : (h + 1) * HEAD_SIZE
        ].astype(jnp.float32)

    head = lax.broadcasted_iota(jnp.int32, (heads, kv_heads * slots), 0)
    column = lax.broadcasted_iota(jnp.int32, (heads, kv_heads * slots), 1)
    position = jnp.where(head // group == column // slots, lax.rem(column, slots), slots)

    def grouped(ref, row):
        parts = [ref[row : row + 1, g * HEAD_SIZE : (g + 1) * HEAD_SIZE] for g in range(kv_heads)]
        return jnp.concatenate(
            [jnp.broadcast_to(part, (group, HEAD_SIZE)) for part in parts], axis=0
        )

    def stacked(ref, b, r):
        return jnp.concatenate(
            [ref[b, r, :, g * HEAD_SIZE : (g + 1) * HEAD_SIZE] for g in range(kv_heads)], axis=0
        )

    def attend(row):
        b, r = divmod(row, rows)
        picked = pl.ds(row, heads, stride=block)
        q = q_rows[picked, :]
        score = lax.dot_general(
            q.astype(jnp.bfloat16),
            stacked(keys, b, r),
            (((1,), (1,)), ((), ())),
            preferred_element_type=jnp.float32,
        )
        score = jnp.where(position < lengths_ref[b, r], score * scale, -jnp.inf)
        own_score = jnp.sum(q * grouped(own_keys, row), axis=1, keepdims=True) * scale
        top = jnp.maximum(jnp.max(score, axis=1, keepdims=True), own_score)
        raised = jnp.exp(score - top)
        own_raised = jnp.exp(own_score - top)
        share = 1.0 / (jnp.sum(raised, axis=1, keepdims=True) + own_raised)
        probs = (raised * share).astype(jnp.bfloat16)
        own_prob = (own_raised * share).astype(jnp.bfloat16).astype(jnp.float32)
        out = jnp.dot(probs, stacked(values, b, r), preferred_element_type=jnp.float32)
        o_rows[picked, :] = out + own_prob * grouped(own_values, row)

    todo = list(range(block))

    def attend_some(count):
        for _ in range(min(count, len(todo))):
            attend(todo.pop(0))

    for step in from_near:
        gather_z(step).wait_recv()
        gather_x(step).start()
        gather_c(0, step).start()
        attend_some(2)
    for turn, step in enumerate([0] + from_near):
        gather_x(step).wait_recv()
        gather_c(1, step).start()
        if turn % 2:
            attend_some(2)

    expert = me // PAIR

    def hidden_units(far_core):
        span = pl.ds(far_core * half, half)
        x = gathered[span, 0:width]
        gate_val = jnp.dot(x, w_gate[0], preferred_element_type=jnp.float32)
        up_val = jnp.dot(x, w_up[0], preferred_element_type=jnp.float32)
        act[span, :] = (gate_val / (1.0 + jnp.exp(-gate_val)) * up_val).astype(jnp.bfloat16)
        tail = gathered[span, width:].astype(jnp.float32)
        at = lax.broadcasted_iota(jnp.int32, tail.shape, 1)
        mine = jnp.sum(jnp.where(lax.rem(at, experts) == expert, tail, 0.0), axis=1, keepdims=True)
        row_weight[span, :] = jnp.broadcast_to(mine, (half, LANES))

    loads[8].wait()
    loads[9].wait()
    hidden_units(0)
    for far_side in range(PAIR):
        for step in range(ring):
            gather_c(far_side, step).wait_recv()
    hidden_units(1)
    loads[10].wait()

    def reduce_c(j):
        return remote(send_c.at[j], recv_c.at[j], rc_send.at[j], rc_recv.at[j], mate)

    def reduce_x(j):
        return remote(send_x.at[j], recv_x.at[j], rx_send.at[j], rx_recv.at[j], side)

    def reduce_z(j, step):
        at = j * ring + step
        return remote(
            send_z.at[j, step], recv_z.at[j, step], rz_send.at[at], rz_recv.at[at], down_by(step)
        )

    def project(j):
        columns = slice(j * chunk, (j + 1) * chunk)
        for far_core in (1, 0):
            span = pl.ds(far_core * half, half)
            out = jnp.dot(act[span, :], w_down[0, :, columns], preferred_element_type=jnp.float32)
            out = out * jnp.concatenate([row_weight[span, :]] * (chunk // LANES), axis=1)
            if far_core:
                send_c[j] = out.astype(jnp.bfloat16)
                reduce_c(j).start()
            else:
                keep_c[j] = out

    def after_c(j):
        reduce_c(j).wait_recv()
        for far_side in (1, 0):
            span = slice(far_side * quarter, (far_side + 1) * quarter)
            out = keep_c[j, span, :] + recv_c[j, span, :].astype(jnp.float32)
            if far_side:
                send_x[j] = out.astype(jnp.bfloat16)
                reduce_x(j).start()
            else:
                keep_x[j] = out

    def after_x(j):
        reduce_x(j).wait_recv()
        for step in order + [0]:
            span = slice(step * block, (step + 1) * block)
            out = keep_x[j, span, :] + recv_x[j, span, :].astype(jnp.float32)
            if step:
                send_z[j, step] = out.astype(jnp.bfloat16)
                reduce_z(j, step).start()
            else:
                keep_x[j, span, :] = out

    def after_z(j):
        out = keep_x[j, 0:block, :]
        for step in order:
            reduce_z(j, step).wait_recv()
            out = out + recv_z[j, step].astype(jnp.float32)
        moe_ref[:, j * chunk : (j + 1) * chunk] = out.astype(jnp.bfloat16)

    for tick in range(chunks + 2):
        if tick < chunks:
            project(tick)
        if tick >= 2:
            after_c(tick - 2)
    attend_some(2)
    for j in range(chunks):
        after_x(j)
        if j % 2 == 0:
            attend_some(2)
    attend_some(block)
    for h in range(heads):
        attn_ref[:, h * HEAD_SIZE : (h + 1) * HEAD_SIZE] = o_rows[
            h * block : (h + 1) * block, :
        ].astype(jnp.bfloat16)
    store_attn = pltpu.make_async_copy(attn_ref, attn_hbm, load_sems.at[11])
    store_attn.start()
    for j in range(chunks):
        after_z(j)
    store_moe = pltpu.make_async_copy(moe_ref, moe_hbm, load_sems.at[12])
    store_moe.start()

    for step in order:
        gather_z(step).wait_send()
    for step in range(ring):
        gather_x(step).wait_send()
        for far_side in range(PAIR):
            gather_c(far_side, step).wait_send()
    for j in range(chunks):
        reduce_c(j).wait_send()
        reduce_x(j).wait_send()
        for step in order:
            reduce_z(j, step).wait_send()
    store_attn.wait()
    store_moe.wait()


def finish_kernel(attn_in, moe_in, attn_out, moe_out, sems):
    copies = [pltpu.make_async_copy(moe_in, moe_out, sems.at[0])]
    pieces = sems.shape[0] - 1
    size = attn_in.shape[1] // pieces
    for i in range(pieces):
        span = pl.ds(i * size, size)
        copies.append(
            pltpu.make_async_copy(attn_in.at[:, span], attn_out.at[:, span], sems.at[1 + i])
        )
    for copy in copies:
        copy.start()
    for copy in copies:
        copy.wait()


def finished(attn_out, moe_out):
    hbm = pl.BlockSpec(memory_space=pl.ANY)
    return pl.pallas_call(
        finish_kernel,
        out_shape=(
            jax.ShapeDtypeStruct(attn_out.shape, attn_out.dtype),
            jax.ShapeDtypeStruct(moe_out.shape, moe_out.dtype),
        ),
        in_specs=[hbm, hbm],
        out_specs=(hbm, hbm),
        scratch_shapes=[pltpu.SemaphoreType.DMA((5,))],
        compiler_params=pltpu.CompilerParams(vmem_limit_bytes=63 * 1024 * 1024),
    )(attn_out, moe_out)


def dense_shards(
    hidden_in,
    routes,
    gates,
    query,
    cached_key_rows,
    cached_value_rows,
    fresh_key,
    fresh_value,
    lengths,
    w_gate,
    w_up,
    w_down,
):
    ep_size = lax.axis_size("ep")
    experts = ep_size // PAIR
    ring = ep_size // (PAIR * PAIR)
    batches, rows, width = hidden_in.shape
    slots = cached_key_rows.shape[2]
    kv_heads = cached_key_rows.shape[3] // HEAD_SIZE
    heads = query.shape[2] // HEAD_SIZE
    depth = w_gate.shape[2]
    chunks = 8
    chunk = width // chunks
    block = batches * rows
    quarter = ring * block
    half = PAIR * quarter
    spread = -(-2 * experts // LANES) * LANES
    dims = (batches, rows, width, heads, kv_heads, slots, experts, depth, chunks, chunk)
    smem = pl.BlockSpec(memory_space=pltpu.SMEM)
    hbm = pl.BlockSpec(memory_space=pl.ANY)
    bf16, f32 = jnp.bfloat16, jnp.float32
    dma = pltpu.SemaphoreType.DMA
    def flat(array):
        return array.reshape(block, array.shape[2])

    attn_out, moe_out = pl.pallas_call(
        functools.partial(layer_kernel, dims),
        out_shape=(
            jax.ShapeDtypeStruct((block, query.shape[2]), bf16),
            jax.ShapeDtypeStruct((block, width), bf16),
        ),
        in_specs=[smem] + [hbm] * 11,
        out_specs=(hbm, hbm),
        scratch_shapes=[
            pltpu.VMEM((block, query.shape[2]), bf16),
            pltpu.VMEM((block, width), bf16),
            pltpu.VMEM((block, width), bf16),
            pltpu.VMEM(routes.shape, jnp.int32),
            pltpu.VMEM(gates.shape, f32),
            pltpu.VMEM((block, query.shape[2]), bf16),
            pltpu.VMEM((block, fresh_key.shape[2]), bf16),
            pltpu.VMEM((block, fresh_value.shape[2]), bf16),
            pltpu.VMEM(cached_key_rows.shape, bf16),
            pltpu.VMEM(cached_value_rows.shape, bf16),
            pltpu.VMEM(w_gate.shape, bf16),
            pltpu.VMEM(w_up.shape, bf16),
            pltpu.VMEM(w_down.shape, bf16),
            pltpu.VMEM((PAIR * half, width + spread), bf16),
            pltpu.VMEM((heads * block, HEAD_SIZE), f32),
            pltpu.VMEM((heads * block, HEAD_SIZE), f32),
            pltpu.VMEM((block, fresh_key.shape[2]), f32),
            pltpu.VMEM((block, fresh_value.shape[2]), f32),
            pltpu.VMEM((PAIR * half, LANES), f32),
            pltpu.VMEM((PAIR * half, depth), bf16),
            pltpu.VMEM((chunks, half, chunk), f32),
            pltpu.VMEM((chunks, quarter, chunk), f32),
            pltpu.VMEM((chunks, half, chunk), bf16),
            pltpu.VMEM((chunks, half, chunk), bf16),
            pltpu.VMEM((chunks, quarter, chunk), bf16),
            pltpu.VMEM((chunks, quarter, chunk), bf16),
            pltpu.VMEM((chunks, ring, block, chunk), bf16),
            pltpu.VMEM((chunks, ring, block, chunk), bf16),
            dma((13,)),
            dma((ring,)),
            dma((ring,)),
            dma((ring,)),
            dma((ring,)),
            dma((PAIR * ring,)),
            dma((PAIR * ring,)),
            dma((chunks,)),
            dma((chunks,)),
            dma((chunks,)),
            dma((chunks,)),
            dma((chunks * ring,)),
            dma((chunks * ring,)),
        ],
        compiler_params=pltpu.CompilerParams(
            collective_id=0, has_side_effects=True, vmem_limit_bytes=63 * 1024 * 1024
        ),
        cost_estimate=pl.CostEstimate(
            flops=6 * PAIR * half * width * depth, bytes_accessed=8 * 1024 * 1024, transcendentals=0
        ),
    )(
        lengths,
        flat(hidden_in),
        routes,
        gates,
        flat(query),
        flat(fresh_key),
        flat(fresh_value),
        cached_key_rows,
        cached_value_rows,
        w_gate,
        w_up,
        w_down,
    )
    attn_out, moe_out = finished(attn_out, moe_out)
    return attn_out.reshape(query.shape), moe_out.reshape(hidden_in.shape)


def shards(*args):
    hidden_in, routes = args[0], args[1]
    ep_size = lax.axis_size("ep")
    batches, rows, width = hidden_in.shape
    every_expert = routes.shape[2] == ep_size // PAIR
    fits = ep_size % (PAIR * PAIR) == 0 and ep_size > PAIR * PAIR and lax.axis_size("tp") == 1
    tiles = batches * rows % TILE_ROWS == 0 and rows % 8 == 0 and width % (8 * LANES) == 0
    if every_expert and fits and tiles:
        return dense_shards(*args)
    return sparse_shards(*args)


def solution(mesh):
    in_specs = (
        P(None, ("grp", "ep"), None),
        P(None, ("grp", "ep"), None),
        P(None, ("grp", "ep"), None),
        P(None, ("grp", "ep"), "tp"),
        P(None, ("grp", "ep"), None, "tp"),
        P(None, ("grp", "ep"), None, "tp"),
        P(None, ("grp", "ep"), "tp"),
        P(None, ("grp", "ep"), "tp"),
        P(None, ("grp", "ep")),
        P("ep", None, "tp"),
        P("ep", None, "tp"),
        P("ep", "tp", None),
    )
    out_specs = (P(None, ("grp", "ep"), "tp"), P(None, ("grp", "ep"), "tp"))
    return jax.shard_map(shards, mesh=mesh, in_specs=in_specs, out_specs=out_specs, check_vma=False)
```

```python
import functools
import math

import jax
import jax.numpy as jnp
from jax import lax
from jax.experimental import pallas as pl
from jax.experimental.pallas import tpu as pltpu
from jax.sharding import PartitionSpec as P

QUERY_HEADS = 64
KEY_VALUE_HEADS = 4
HEAD_SIZE = 128


def swapped(block, axis, bit):
    count = lax.axis_size(axis)
    route = []
    for low in range(count):
        high = low | 1 << bit
        if high != low and high < count:
            route += [(low, high), (high, low)]
    return lax.ppermute(block, axis, route)


def attend_local(query_rows, cached_key_rows, cached_value_rows, fresh_key, fresh_value, lengths):
    row_count = query_rows.shape[0]
    query_group = QUERY_HEADS // KEY_VALUE_HEADS
    kv_local = cached_key_rows.shape[2] // HEAD_SIZE
    cache_len = cached_key_rows.shape[1]
    grouped_query_rows = query_rows.reshape(row_count, kv_local, query_group, HEAD_SIZE)
    earlier_keys = cached_key_rows.reshape(row_count, cache_len, kv_local, HEAD_SIZE)
    earlier_values = cached_value_rows.reshape(row_count, cache_len, kv_local, HEAD_SIZE)
    token_own_keys = fresh_key.reshape(row_count, kv_local, HEAD_SIZE)
    token_own_values = fresh_value.reshape(row_count, kv_local, HEAD_SIZE).astype(jnp.float32)
    score_scale = 1.0 / math.sqrt(HEAD_SIZE)
    past_score = (
        jnp.einsum(
            "rkgd,rckd->rkgc", grouped_query_rows, earlier_keys, preferred_element_type=jnp.float32
        )
        * score_scale
    )
    own_score = (
        jnp.einsum(
            "rkgd,rkd->rkg", grouped_query_rows, token_own_keys, preferred_element_type=jnp.float32
        )[..., None]
        * score_scale
    )
    valid_pos = lax.broadcasted_iota(jnp.int32, (row_count, cache_len), 1) < lengths[:, None]
    past_score = jnp.where(valid_pos[:, None, None, :], past_score, -jnp.inf)
    scores = jnp.concatenate([past_score, own_score], axis=-1)
    row_max = jnp.max(scores, axis=-1, keepdims=True)
    exp_scores = jnp.exp(scores - row_max)
    weights_bf = (exp_scores / jnp.sum(exp_scores, axis=-1, keepdims=True)).astype(jnp.bfloat16)
    attended = jnp.einsum(
        "rkgc,rckd->rkgd",
        weights_bf[..., :cache_len],
        earlier_values,
        preferred_element_type=jnp.float32,
    )
    attended = (
        attended + weights_bf[..., cache_len:].astype(jnp.float32) * token_own_values[:, :, None, :]
    )
    return attended.reshape(row_count, kv_local * query_group * HEAD_SIZE).astype(jnp.bfloat16)


def slot_layout(route_rows, experts, capacity):
    flat_routes = route_rows.reshape(-1)
    onehot = (flat_routes[:, None] == jnp.arange(experts, dtype=jnp.int32)[None, :]).astype(
        jnp.int32
    )
    before = jnp.cumsum(onehot, axis=0) - onehot
    slot_rank = jnp.sum(before * onehot, axis=1)
    return 2 * flat_routes * capacity + slot_rank


def pack_rows(tokens, first_slot, capacity, slot_total, route_count):
    targets = jnp.stack([first_slot, first_slot + capacity], axis=1)
    slot_ids = lax.broadcasted_iota(jnp.int32, (slot_total, 1, 1), 0)
    chosen = jnp.sum((targets[None, :, :] == slot_ids).astype(jnp.float32), axis=2)
    chosen = jnp.sum(chosen.reshape(slot_total, -1, route_count), axis=2).astype(jnp.bfloat16)
    return jnp.dot(chosen, tokens, preferred_element_type=jnp.float32).astype(jnp.bfloat16)


def combine_rows(returned, first_slot, capacity, row_gates, row_count, route_count):
    flat_back = returned.reshape(returned.shape[0] * returned.shape[1], returned.shape[2])
    lower = jnp.take(flat_back, first_slot, axis=0)
    upper = jnp.take(flat_back, first_slot + capacity, axis=0)
    outputs = jnp.concatenate([lower, upper], axis=1)
    outputs = lax.optimization_barrier(outputs).astype(jnp.float32)
    weighted = row_gates.reshape(-1, 1) * outputs
    return jnp.sum(weighted.reshape(row_count, route_count, -1), axis=1).astype(jnp.bfloat16)


def sparse_shards(
    hidden_in,
    routes,
    gates,
    query,
    cached_key_rows,
    cached_value_rows,
    fresh_key,
    fresh_value,
    lengths,
    w_gate,
    w_up,
    w_down,
):
    ep_size = lax.axis_size("ep")
    experts = ep_size // 2
    batches, row_count, route_count = routes.shape
    model_width = hidden_in.shape[2]
    capacity = min(row_count, 2 * ((row_count * route_count + experts - 1) // experts))
    slot_total = ep_size * capacity
    layouts = []
    buffers = []
    for batch_idx in range(batches):
        first_slot = slot_layout(routes[batch_idx], experts, capacity)
        layouts.append(first_slot)
        packed = pack_rows(hidden_in[batch_idx], first_slot, capacity, slot_total, route_count)
        buffers.append(packed.reshape(ep_size, capacity, model_width))
    attn_list = []
    blocks = []
    for batch_idx in range(batches):
        received = lax.all_to_all(buffers[batch_idx], "ep", split_axis=0, concat_axis=0, tiled=True)
        item_count = received.shape[1]
        slot_rows = received.reshape(ep_size * item_count, model_width)
        gate_val = jnp.dot(slot_rows, w_gate[0], preferred_element_type=jnp.float32)
        up_val = jnp.dot(slot_rows, w_up[0], preferred_element_type=jnp.float32)
        hidden = (jax.nn.silu(gate_val) * up_val).astype(jnp.bfloat16)
        partial_value = jnp.dot(hidden, w_down[0], preferred_element_type=jnp.float32)
        partial_value = partial_value.reshape(ep_size, item_count, model_width)
        half_sum = lax.psum_scatter(partial_value, "tp", scatter_dimension=2, tiled=True)
        partner = swapped(half_sum, "ep", 0)
        finished = (half_sum + partner).astype(jnp.bfloat16)
        quarter = finished.shape[2] // 2
        parity = lax.axis_index("ep") % 2
        quarter_cols = lax.dynamic_slice_in_dim(finished, parity * quarter, quarter, 2)
        blocks.append(lax.all_to_all(quarter_cols, "ep", split_axis=0, concat_axis=0, tiled=True))
        attn_list.append(
            attend_local(
                query[batch_idx],
                cached_key_rows[batch_idx],
                cached_value_rows[batch_idx],
                fresh_key[batch_idx],
                fresh_value[batch_idx],
                lengths[batch_idx],
            )
        )
    moe_list = []
    for batch_idx in range(batches):
        moe_list.append(
            combine_rows(
                blocks[batch_idx],
                layouts[batch_idx],
                capacity,
                gates[batch_idx],
                row_count,
                route_count,
            )
        )
    return (jnp.stack(attn_list), jnp.stack(moe_list))


LANES = 128
TILE_ROWS = 16
PAIR = 2
MESH = pl.DeviceIdType.MESH


def remote(src, dst, send_sem, recv_sem, index):
    return pltpu.make_async_remote_copy(
        src_ref=src,
        dst_ref=dst,
        send_sem=send_sem,
        recv_sem=recv_sem,
        device_id={"ep": index},
        device_id_type=MESH,
    )


def layer_kernel(
    dims,
    lengths_ref,
    hidden_hbm,
    routes_hbm,
    gates_hbm,
    query_hbm,
    fresh_key_hbm,
    fresh_value_hbm,
    key_hbm,
    value_hbm,
    gate_hbm,
    up_hbm,
    down_hbm,
    attn_hbm,
    moe_hbm,
    attn_ref,
    moe_ref,
    hidden_ref,
    routes_ref,
    gates_ref,
    query_ref,
    fresh_key_ref,
    fresh_value_ref,
    keys,
    values,
    w_gate,
    w_up,
    w_down,
    gathered,
    q_rows,
    o_rows,
    own_keys,
    own_values,
    row_weight,
    gate_sum,
    up_sum,
    act,
    keep_c,
    keep_x,
    send_c,
    recv_c,
    send_x,
    recv_x,
    send_z,
    recv_z,
    load_sems,
    gz_send,
    gz_recv,
    gx_send,
    gx_recv,
    gc_send,
    gc_recv,
    rc_send,
    rc_recv,
    rx_send,
    rx_recv,
    rz_send,
    rz_recv,
):
    batches, rows, width, heads, kv_heads, slots, experts, depth, chunks, chunk = dims
    ring = gz_send.shape[1]
    block = batches * rows
    quarter = ring * block
    half = PAIR * quarter
    group = heads // kv_heads
    scale = 1.0 / math.sqrt(HEAD_SIZE)

    me = lax.axis_index("ep")
    core = lax.rem(me, PAIR)
    across = lax.rem(me // PAIR, PAIR)
    place = lax.rem(me, PAIR * PAIR)
    level = me // (PAIR * PAIR)
    mate = me + 1 - PAIR * core
    side = me + PAIR - PAIR * PAIR * across

    def up_by(step):
        return lax.rem(level + step, ring) * (PAIR * PAIR) + place

    shorter = jnp.minimum(level, ring - 1 - level)
    longer = 1 - 2 * (level // ((ring + 1) // 2))

    def nearest(turn):
        distance = jnp.where(turn <= 2 * shorter, (turn + 1) // 2, turn - shorter)
        towards = jnp.where(turn <= 2 * shorter, (2 * (turn % 2) - 1) * longer, longer)
        return lax.rem(distance * towards + ring, ring)

    def down_by(step):
        return lax.rem(level + ring - step, ring) * (PAIR * PAIR) + place

    loads = [
        pltpu.make_async_copy(source, target, load_sems.at[i])
        for i, (source, target) in enumerate(
            (
                (hidden_hbm, hidden_ref),
                (routes_hbm, routes_ref),
                (gates_hbm, gates_ref),
                (query_hbm, query_ref),
                (fresh_key_hbm, fresh_key_ref),
                (fresh_value_hbm, fresh_value_ref),
                (key_hbm, keys),
                (value_hbm, values),
                (gate_hbm, w_gate),
                (up_hbm, w_up),
                (down_hbm, w_down),
            )
        )
    ]
    for load in loads:
        load.start()

    barrier = pltpu.get_barrier_semaphore()
    others = [mate, side] + [up_by(step) for step in range(1, ring)]
    for other in others:
        pl.semaphore_signal(barrier, inc=1, device_id={"ep": other}, device_id_type=MESH)

    for load in loads[0:3]:
        load.wait()
    gathered[0:block, 0:width] = hidden_ref[...]
    spread = gathered.shape[1] - width
    lane = lax.broadcasted_iota(jnp.int32, (rows, spread), 1)
    expert_of = lax.rem(lane, experts)
    tails = []
    for b in range(batches):
        dense = jnp.zeros((rows, spread), jnp.float32)
        for k in range(routes_ref.shape[2]):
            named = routes_ref[b, :, k : k + 1] == expert_of
            dense = dense + jnp.where(named, gates_ref[b, :, k : k + 1], 0.0)
        high = dense.astype(jnp.bfloat16).astype(jnp.float32)
        tail = jnp.where(lane < experts, high, dense - high)
        tails.append(jnp.where(lane < 2 * experts, tail, 0.0))
    gathered[0:block, width:] = jnp.concatenate(tails, axis=0).astype(jnp.bfloat16)

    pl.semaphore_wait(barrier, len(others))

    def slot(far_core, far_side, step):
        start = ((far_core * PAIR + far_side) * ring + step) * block
        return pl.ds(pl.multiple_of(start, block), block)

    cuts = (slice(0, width // 2), slice(width // 2, gathered.shape[1]))

    def part_of(rows_at, part):
        size = cuts[part].stop - cuts[part].start
        return gathered.at[rows_at, pl.ds(cuts[part].start, size)]

    def gather_z(part, step):
        return remote(
            part_of(slot(0, 0, 0), part),
            part_of(slot(0, 0, step), part),
            gz_send.at[part, step],
            gz_recv.at[part, step],
            up_by(step),
        )

    def gather_x(part, step):
        return remote(
            part_of(slot(0, 0, step), part),
            part_of(slot(0, 1, step), part),
            gx_send.at[part, step],
            gx_recv.at[part, step],
            side,
        )

    def gather_c(part, far_side, step):
        return remote(
            part_of(slot(0, far_side, step), part),
            part_of(slot(1, far_side, step), part),
            gc_send.at[part, far_side * ring + step],
            gc_recv.at[part, far_side * ring + step],
            mate,
        )

    order = list(range(1, ring))
    to_near = [nearest(turn) for turn in order]
    from_near = [lax.rem(ring - step, ring) for step in to_near]
    for part in range(2):
        for step in to_near:
            gather_z(part, step).start()
        gather_x(part, 0).start()
        gather_c(part, 0, 0).start()

    for load in loads[3:8]:
        load.wait()
    own_keys[...] = fresh_key_ref[...].astype(jnp.float32)
    own_values[...] = fresh_value_ref[...].astype(jnp.float32)
    for h in range(heads):
        q_rows[h * block : (h + 1) * block, :] = query_ref[
            :, h * HEAD_SIZE : (h + 1) * HEAD_SIZE
        ].astype(jnp.float32)

    head = lax.broadcasted_iota(jnp.int32, (heads, kv_heads * slots), 0)
    column = lax.broadcasted_iota(jnp.int32, (heads, kv_heads * slots), 1)
    position = jnp.where(head // group == column // slots, lax.rem(column, slots), slots)

    def grouped(ref, row):
        parts = [ref[row : row + 1, g * HEAD_SIZE : (g + 1) * HEAD_SIZE] for g in range(kv_heads)]
        return jnp.concatenate(
            [jnp.broadcast_to(part, (group, HEAD_SIZE)) for part in parts], axis=0
        )

    def stacked(ref, b, r):
        return jnp.concatenate(
            [ref[b, r, :, g * HEAD_SIZE : (g + 1) * HEAD_SIZE] for g in range(kv_heads)], axis=0
        )

    def attend(row):
        b, r = divmod(row, rows)
        picked = pl.ds(row, heads, stride=block)
        q = q_rows[picked, :]
        score = lax.dot_general(
            q.astype(jnp.bfloat16),
            stacked(keys, b, r),
            (((1,), (1,)), ((), ())),
            preferred_element_type=jnp.float32,
        )
        score = jnp.where(position < lengths_ref[b, r], score * scale, -jnp.inf)
        own_score = jnp.sum(q * grouped(own_keys, row), axis=1, keepdims=True) * scale
        top = jnp.maximum(jnp.max(score, axis=1, keepdims=True), own_score)
        raised = jnp.exp(score - top)
        own_raised = jnp.exp(own_score - top)
        share = 1.0 / (jnp.sum(raised, axis=1, keepdims=True) + own_raised)
        probs = (raised * share).astype(jnp.bfloat16)
        own_prob = (own_raised * share).astype(jnp.bfloat16).astype(jnp.float32)
        out = jnp.dot(probs, stacked(values, b, r), preferred_element_type=jnp.float32)
        o_rows[picked, :] = out + own_prob * grouped(own_values, row)

    todo = list(range(block))

    def attend_some(count):
        for _ in range(min(count, len(todo))):
            attend(todo.pop(0))

    def forward_z(part, step):
        gather_z(part, step).wait_recv()
        gather_x(part, step).start()
        gather_c(part, 0, step).start()

    def forward_x(part, step):
        gather_x(part, step).wait_recv()
        gather_c(part, 1, step).start()

    def arrived(part):
        for far_side in range(PAIR):
            for step in range(ring):
                gather_c(part, far_side, step).wait_recv()

    def units(part):
        columns = slice(part * (width // 2), (part + 1) * (width // 2))
        x = gathered[:, columns]
        return (
            jnp.dot(x, w_gate[0, columns, :], preferred_element_type=jnp.float32),
            jnp.dot(x, w_up[0, columns, :], preferred_element_type=jnp.float32),
        )

    for step in from_near:
        forward_z(0, step)
        attend_some(2)
    for turn, step in enumerate([0] + from_near):
        forward_x(0, step)
    for step in from_near:
        forward_z(1, step)
    attend_some(2)
    loads[8].wait()
    loads[9].wait()
    arrived(0)
    gate_sum[...], up_sum[...] = units(0)
    for step in [0] + from_near:
        forward_x(1, step)
    arrived(1)
    gate_val, up_val = units(1)
    gate_val = gate_val + gate_sum[...]
    up_val = up_val + up_sum[...]
    act[...] = (gate_val / (1.0 + jnp.exp(-gate_val)) * up_val).astype(jnp.bfloat16)
    tail = gathered[:, width:].astype(jnp.float32)
    at = lax.broadcasted_iota(jnp.int32, tail.shape, 1)
    mine = jnp.where(lax.rem(at, experts) == me // PAIR, tail, 0.0)
    row_weight[...] = jnp.broadcast_to(jnp.sum(mine, axis=1, keepdims=True), row_weight.shape)
    loads[10].wait()

    def reduce_c(j):
        return remote(send_c.at[j], recv_c.at[j], rc_send.at[j], rc_recv.at[j], mate)

    def reduce_x(j):
        return remote(send_x.at[j], recv_x.at[j], rx_send.at[j], rx_recv.at[j], side)

    def reduce_z(j, step):
        at = j * ring + step
        return remote(
            send_z.at[j, step], recv_z.at[j, step], rz_send.at[at], rz_recv.at[at], down_by(step)
        )

    def project(j):
        columns = slice(j * chunk, (j + 1) * chunk)
        for far_core in (1, 0):
            span = pl.ds(far_core * half, half)
            out = jnp.dot(act[span, :], w_down[0, :, columns], preferred_element_type=jnp.float32)
            out = out * jnp.concatenate([row_weight[span, :]] * (chunk // LANES), axis=1)
            if far_core:
                send_c[j] = out.astype(jnp.bfloat16)
                reduce_c(j).start()
            else:
                keep_c[j] = out

    def after_c(j):
        reduce_c(j).wait_recv()
        for far_side in (1, 0):
            span = slice(far_side * quarter, (far_side + 1) * quarter)
            out = keep_c[j, span, :] + recv_c[j, span, :].astype(jnp.float32)
            if far_side:
                send_x[j] = out.astype(jnp.bfloat16)
                reduce_x(j).start()
            else:
                keep_x[j] = out

    def after_x(j):
        reduce_x(j).wait_recv()
        for step in order + [0]:
            span = slice(step * block, (step + 1) * block)
            out = keep_x[j, span, :] + recv_x[j, span, :].astype(jnp.float32)
            if step:
                send_z[j, step] = out.astype(jnp.bfloat16)
                reduce_z(j, step).start()
            else:
                keep_x[j, span, :] = out

    def after_z(j):
        out = keep_x[j, 0:block, :]
        for step in order:
            reduce_z(j, step).wait_recv()
            out = out + recv_z[j, step].astype(jnp.float32)
        moe_ref[:, j * chunk : (j + 1) * chunk] = out.astype(jnp.bfloat16)

    for tick in range(chunks + 2):
        if tick < chunks:
            project(tick)
        if tick >= 2:
            after_c(tick - 2)
    attend_some(2)
    for j in range(chunks):
        after_x(j)
        if j % 2 == 0:
            attend_some(2)
    attend_some(block)
    for h in range(heads):
        attn_ref[:, h * HEAD_SIZE : (h + 1) * HEAD_SIZE] = o_rows[
            h * block : (h + 1) * block, :
        ].astype(jnp.bfloat16)
    store_attn = pltpu.make_async_copy(attn_ref, attn_hbm, load_sems.at[11])
    store_attn.start()
    for j in range(chunks):
        after_z(j)
    store_moe = pltpu.make_async_copy(moe_ref, moe_hbm, load_sems.at[12])
    store_moe.start()

    for part in range(2):
        for step in order:
            gather_z(part, step).wait_send()
        for step in range(ring):
            gather_x(part, step).wait_send()
            for far_side in range(PAIR):
                gather_c(part, far_side, step).wait_send()
    for j in range(chunks):
        reduce_c(j).wait_send()
        reduce_x(j).wait_send()
        for step in order:
            reduce_z(j, step).wait_send()
    store_attn.wait()
    store_moe.wait()


def finish_kernel(attn_in, moe_in, attn_out, moe_out):
    attn_out[...] = attn_in[...]
    moe_out[...] = moe_in[...]


def finished(attn_out, moe_out):
    vmem = pl.BlockSpec(memory_space=pltpu.VMEM)
    return pl.pallas_call(
        finish_kernel,
        out_shape=(
            jax.ShapeDtypeStruct(attn_out.shape, attn_out.dtype),
            jax.ShapeDtypeStruct(moe_out.shape, moe_out.dtype),
        ),
        in_specs=[vmem, vmem],
        out_specs=(vmem, vmem),
        compiler_params=pltpu.CompilerParams(vmem_limit_bytes=63 * 1024 * 1024),
    )(attn_out, moe_out)


def dense_shards(
    hidden_in,
    routes,
    gates,
    query,
    cached_key_rows,
    cached_value_rows,
    fresh_key,
    fresh_value,
    lengths,
    w_gate,
    w_up,
    w_down,
):
    ep_size = lax.axis_size("ep")
    experts = ep_size // PAIR
    ring = ep_size // (PAIR * PAIR)
    batches, rows, width = hidden_in.shape
    slots = cached_key_rows.shape[2]
    kv_heads = cached_key_rows.shape[3] // HEAD_SIZE
    heads = query.shape[2] // HEAD_SIZE
    depth = w_gate.shape[2]
    chunks = 8
    chunk = width // chunks
    block = batches * rows
    quarter = ring * block
    half = PAIR * quarter
    spread = -(-2 * experts // LANES) * LANES
    dims = (batches, rows, width, heads, kv_heads, slots, experts, depth, chunks, chunk)
    smem = pl.BlockSpec(memory_space=pltpu.SMEM)
    hbm = pl.BlockSpec(memory_space=pl.ANY)
    bf16, f32 = jnp.bfloat16, jnp.float32
    dma = pltpu.SemaphoreType.DMA
    def flat(array):
        return array.reshape(block, array.shape[2])

    attn_out, moe_out = pl.pallas_call(
        functools.partial(layer_kernel, dims),
        out_shape=(
            jax.ShapeDtypeStruct((block, query.shape[2]), bf16),
            jax.ShapeDtypeStruct((block, width), bf16),
        ),
        in_specs=[smem] + [hbm] * 11,
        out_specs=(hbm, hbm),
        scratch_shapes=[
            pltpu.VMEM((block, query.shape[2]), bf16),
            pltpu.VMEM((block, width), bf16),
            pltpu.VMEM((block, width), bf16),
            pltpu.VMEM(routes.shape, jnp.int32),
            pltpu.VMEM(gates.shape, f32),
            pltpu.VMEM((block, query.shape[2]), bf16),
            pltpu.VMEM((block, fresh_key.shape[2]), bf16),
            pltpu.VMEM((block, fresh_value.shape[2]), bf16),
            pltpu.VMEM(cached_key_rows.shape, bf16),
            pltpu.VMEM(cached_value_rows.shape, bf16),
            pltpu.VMEM(w_gate.shape, bf16),
            pltpu.VMEM(w_up.shape, bf16),
            pltpu.VMEM(w_down.shape, bf16),
            pltpu.VMEM((PAIR * half, width + spread), bf16),
            pltpu.VMEM((heads * block, HEAD_SIZE), f32),
            pltpu.VMEM((heads * block, HEAD_SIZE), f32),
            pltpu.VMEM((block, fresh_key.shape[2]), f32),
            pltpu.VMEM((block, fresh_value.shape[2]), f32),
            pltpu.VMEM((PAIR * half, LANES), f32),
            pltpu.VMEM((PAIR * half, depth), f32),
            pltpu.VMEM((PAIR * half, depth), f32),
            pltpu.VMEM((PAIR * half, depth), bf16),
            pltpu.VMEM((chunks, half, chunk), f32),
            pltpu.VMEM((chunks, quarter, chunk), f32),
            pltpu.VMEM((chunks, half, chunk), bf16),
            pltpu.VMEM((chunks, half, chunk), bf16),
            pltpu.VMEM((chunks, quarter, chunk), bf16),
            pltpu.VMEM((chunks, quarter, chunk), bf16),
            pltpu.VMEM((chunks, ring, block, chunk), bf16),
            pltpu.VMEM((chunks, ring, block, chunk), bf16),
            dma((13,)),
            dma((2, ring)),
            dma((2, ring)),
            dma((2, ring)),
            dma((2, ring)),
            dma((2, PAIR * ring)),
            dma((2, PAIR * ring)),
            dma((chunks,)),
            dma((chunks,)),
            dma((chunks,)),
            dma((chunks,)),
            dma((chunks * ring,)),
            dma((chunks * ring,)),
        ],
        compiler_params=pltpu.CompilerParams(
            collective_id=0, has_side_effects=True, vmem_limit_bytes=63 * 1024 * 1024
        ),
        cost_estimate=pl.CostEstimate(
            flops=6 * PAIR * half * width * depth, bytes_accessed=8 * 1024 * 1024, transcendentals=0
        ),
    )(
        lengths,
        flat(hidden_in),
        routes,
        gates,
        flat(query),
        flat(fresh_key),
        flat(fresh_value),
        cached_key_rows,
        cached_value_rows,
        w_gate,
        w_up,
        w_down,
    )
    attn_out, moe_out = finished(attn_out, moe_out)
    return attn_out.reshape(query.shape), moe_out.reshape(hidden_in.shape)


def shards(*args):
    hidden_in, routes = args[0], args[1]
    ep_size = lax.axis_size("ep")
    batches, rows, width = hidden_in.shape
    every_expert = routes.shape[2] == ep_size // PAIR
    fits = ep_size % (PAIR * PAIR) == 0 and ep_size > PAIR * PAIR and lax.axis_size("tp") == 1
    tiles = batches * rows % TILE_ROWS == 0 and rows % 8 == 0 and width % (8 * LANES) == 0
    if every_expert and fits and tiles:
        return dense_shards(*args)
    return sparse_shards(*args)


def solution(mesh):
    in_specs = (
        P(None, ("grp", "ep"), None),
        P(None, ("grp", "ep"), None),
        P(None, ("grp", "ep"), None),
        P(None, ("grp", "ep"), "tp"),
        P(None, ("grp", "ep"), None, "tp"),
        P(None, ("grp", "ep"), None, "tp"),
        P(None, ("grp", "ep"), "tp"),
        P(None, ("grp", "ep"), "tp"),
        P(None, ("grp", "ep")),
        P("ep", None, "tp"),
        P("ep", None, "tp"),
        P("ep", "tp", None),
    )
    out_specs = (P(None, ("grp", "ep"), "tp"), P(None, ("grp", "ep"), "tp"))
    return jax.shard_map(shards, mesh=mesh, in_specs=in_specs, out_specs=out_specs, check_vma=False)
```

```python
import functools
import math

import jax
import jax.numpy as jnp
from jax import lax
from jax.experimental import pallas as pl
from jax.experimental.pallas import tpu as pltpu
from jax.sharding import PartitionSpec as P

QUERY_HEADS = 64
KEY_VALUE_HEADS = 4
HEAD_SIZE = 128


def swapped(block, axis, bit):
    count = lax.axis_size(axis)
    route = []
    for low in range(count):
        high = low | 1 << bit
        if high != low and high < count:
            route += [(low, high), (high, low)]
    return lax.ppermute(block, axis, route)


def attend_local(query_rows, cached_key_rows, cached_value_rows, fresh_key, fresh_value, lengths):
    row_count = query_rows.shape[0]
    query_group = QUERY_HEADS // KEY_VALUE_HEADS
    kv_local = cached_key_rows.shape[2] // HEAD_SIZE
    cache_len = cached_key_rows.shape[1]
    grouped_query_rows = query_rows.reshape(row_count, kv_local, query_group, HEAD_SIZE)
    earlier_keys = cached_key_rows.reshape(row_count, cache_len, kv_local, HEAD_SIZE)
    earlier_values = cached_value_rows.reshape(row_count, cache_len, kv_local, HEAD_SIZE)
    token_own_keys = fresh_key.reshape(row_count, kv_local, HEAD_SIZE)
    token_own_values = fresh_value.reshape(row_count, kv_local, HEAD_SIZE).astype(jnp.float32)
    score_scale = 1.0 / math.sqrt(HEAD_SIZE)
    past_score = (
        jnp.einsum(
            "rkgd,rckd->rkgc", grouped_query_rows, earlier_keys, preferred_element_type=jnp.float32
        )
        * score_scale
    )
    own_score = (
        jnp.einsum(
            "rkgd,rkd->rkg", grouped_query_rows, token_own_keys, preferred_element_type=jnp.float32
        )[..., None]
        * score_scale
    )
    valid_pos = lax.broadcasted_iota(jnp.int32, (row_count, cache_len), 1) < lengths[:, None]
    past_score = jnp.where(valid_pos[:, None, None, :], past_score, -jnp.inf)
    scores = jnp.concatenate([past_score, own_score], axis=-1)
    row_max = jnp.max(scores, axis=-1, keepdims=True)
    exp_scores = jnp.exp(scores - row_max)
    weights_bf = (exp_scores / jnp.sum(exp_scores, axis=-1, keepdims=True)).astype(jnp.bfloat16)
    attended = jnp.einsum(
        "rkgc,rckd->rkgd",
        weights_bf[..., :cache_len],
        earlier_values,
        preferred_element_type=jnp.float32,
    )
    attended = (
        attended + weights_bf[..., cache_len:].astype(jnp.float32) * token_own_values[:, :, None, :]
    )
    return attended.reshape(row_count, kv_local * query_group * HEAD_SIZE).astype(jnp.bfloat16)


def slot_layout(route_rows, experts, capacity):
    flat_routes = route_rows.reshape(-1)
    onehot = (flat_routes[:, None] == jnp.arange(experts, dtype=jnp.int32)[None, :]).astype(
        jnp.int32
    )
    before = jnp.cumsum(onehot, axis=0) - onehot
    slot_rank = jnp.sum(before * onehot, axis=1)
    return 2 * flat_routes * capacity + slot_rank


def pack_rows(tokens, first_slot, capacity, slot_total, route_count):
    targets = jnp.stack([first_slot, first_slot + capacity], axis=1)
    slot_ids = lax.broadcasted_iota(jnp.int32, (slot_total, 1, 1), 0)
    chosen = jnp.sum((targets[None, :, :] == slot_ids).astype(jnp.float32), axis=2)
    chosen = jnp.sum(chosen.reshape(slot_total, -1, route_count), axis=2).astype(jnp.bfloat16)
    return jnp.dot(chosen, tokens, preferred_element_type=jnp.float32).astype(jnp.bfloat16)


def combine_rows(returned, first_slot, capacity, row_gates, row_count, route_count):
    flat_back = returned.reshape(returned.shape[0] * returned.shape[1], returned.shape[2])
    lower = jnp.take(flat_back, first_slot, axis=0)
    upper = jnp.take(flat_back, first_slot + capacity, axis=0)
    outputs = jnp.concatenate([lower, upper], axis=1)
    outputs = lax.optimization_barrier(outputs).astype(jnp.float32)
    weighted = row_gates.reshape(-1, 1) * outputs
    return jnp.sum(weighted.reshape(row_count, route_count, -1), axis=1).astype(jnp.bfloat16)


def sparse_shards(
    hidden_in,
    routes,
    gates,
    query,
    cached_key_rows,
    cached_value_rows,
    fresh_key,
    fresh_value,
    lengths,
    w_gate,
    w_up,
    w_down,
):
    ep_size = lax.axis_size("ep")
    experts = ep_size // 2
    batches, row_count, route_count = routes.shape
    model_width = hidden_in.shape[2]
    capacity = min(row_count, 2 * ((row_count * route_count + experts - 1) // experts))
    slot_total = ep_size * capacity
    layouts = []
    buffers = []
    for batch_idx in range(batches):
        first_slot = slot_layout(routes[batch_idx], experts, capacity)
        layouts.append(first_slot)
        packed = pack_rows(hidden_in[batch_idx], first_slot, capacity, slot_total, route_count)
        buffers.append(packed.reshape(ep_size, capacity, model_width))
    attn_list = []
    blocks = []
    for batch_idx in range(batches):
        received = lax.all_to_all(buffers[batch_idx], "ep", split_axis=0, concat_axis=0, tiled=True)
        item_count = received.shape[1]
        slot_rows = received.reshape(ep_size * item_count, model_width)
        gate_val = jnp.dot(slot_rows, w_gate[0], preferred_element_type=jnp.float32)
        up_val = jnp.dot(slot_rows, w_up[0], preferred_element_type=jnp.float32)
        hidden = (jax.nn.silu(gate_val) * up_val).astype(jnp.bfloat16)
        partial_value = jnp.dot(hidden, w_down[0], preferred_element_type=jnp.float32)
        partial_value = partial_value.reshape(ep_size, item_count, model_width)
        half_sum = lax.psum_scatter(partial_value, "tp", scatter_dimension=2, tiled=True)
        partner = swapped(half_sum, "ep", 0)
        finished = (half_sum + partner).astype(jnp.bfloat16)
        quarter = finished.shape[2] // 2
        parity = lax.axis_index("ep") % 2
        quarter_cols = lax.dynamic_slice_in_dim(finished, parity * quarter, quarter, 2)
        blocks.append(lax.all_to_all(quarter_cols, "ep", split_axis=0, concat_axis=0, tiled=True))
        attn_list.append(
            attend_local(
                query[batch_idx],
                cached_key_rows[batch_idx],
                cached_value_rows[batch_idx],
                fresh_key[batch_idx],
                fresh_value[batch_idx],
                lengths[batch_idx],
            )
        )
    moe_list = []
    for batch_idx in range(batches):
        moe_list.append(
            combine_rows(
                blocks[batch_idx],
                layouts[batch_idx],
                capacity,
                gates[batch_idx],
                row_count,
                route_count,
            )
        )
    return (jnp.stack(attn_list), jnp.stack(moe_list))


LANES = 128
TILE_ROWS = 16
PAIR = 2
MESH = pl.DeviceIdType.MESH


def remote(src, dst, send_sem, recv_sem, index):
    return pltpu.make_async_remote_copy(
        src_ref=src,
        dst_ref=dst,
        send_sem=send_sem,
        recv_sem=recv_sem,
        device_id={"ep": index},
        device_id_type=MESH,
    )


def layer_kernel(
    dims,
    lengths_ref,
    hidden_hbm,
    routes_hbm,
    gates_hbm,
    query_hbm,
    fresh_key_hbm,
    fresh_value_hbm,
    key_hbm,
    value_hbm,
    gate_hbm,
    up_hbm,
    down_hbm,
    attn_hbm,
    moe_hbm,
    attn_ref,
    moe_ref,
    hidden_ref,
    routes_ref,
    gates_ref,
    query_ref,
    fresh_key_ref,
    fresh_value_ref,
    keys,
    values,
    w_gate,
    w_up,
    w_down,
    gathered,
    q_rows,
    o_rows,
    own_keys,
    own_values,
    row_weight,
    act,
    keep_c,
    keep_x,
    send_c,
    recv_c,
    send_x,
    recv_x,
    send_z,
    recv_z,
    load_sems,
    gz_send,
    gz_recv,
    gx_send,
    gx_recv,
    gc_send,
    gc_recv,
    rc_send,
    rc_recv,
    rx_send,
    rx_recv,
    rz_send,
    rz_recv,
):
    batches, rows, width, heads, kv_heads, slots, experts, depth, chunks, chunk = dims
    ring = gz_send.shape[0]
    block = batches * rows
    quarter = ring * block
    half = PAIR * quarter
    group = heads // kv_heads
    scale = 1.0 / math.sqrt(HEAD_SIZE)

    me = lax.axis_index("ep")
    core = lax.rem(me, PAIR)
    across = lax.rem(me // PAIR, PAIR)
    place = lax.rem(me, PAIR * PAIR)
    level = me // (PAIR * PAIR)
    mate = me + 1 - PAIR * core
    side = me + PAIR - PAIR * PAIR * across

    def up_by(step):
        return lax.rem(level + step, ring) * (PAIR * PAIR) + place

    def down_by(step):
        return lax.rem(level + ring - step, ring) * (PAIR * PAIR) + place

    loads = [
        pltpu.make_async_copy(source, target, load_sems.at[i])
        for i, (source, target) in enumerate(
            (
                (hidden_hbm, hidden_ref),
                (routes_hbm, routes_ref),
                (gates_hbm, gates_ref),
                (query_hbm, query_ref),
                (fresh_key_hbm, fresh_key_ref),
                (fresh_value_hbm, fresh_value_ref),
                (key_hbm, keys),
                (value_hbm, values),
                (gate_hbm, w_gate),
                (up_hbm, w_up),
                (down_hbm, w_down),
            )
        )
    ]
    for load in loads:
        load.start()

    barrier = pltpu.get_barrier_semaphore()
    others = [mate, side] + [up_by(step) for step in range(1, ring)]
    for other in others:
        pl.semaphore_signal(barrier, inc=1, device_id={"ep": other}, device_id_type=MESH)

    for load in loads[0:3]:
        load.wait()
    gathered[0:block, 0:width] = hidden_ref[...]
    spread = gathered.shape[1] - width
    lane = lax.broadcasted_iota(jnp.int32, (rows, spread), 1)
    expert_of = lax.rem(lane, experts)
    tails = []
    for b in range(batches):
        dense = jnp.zeros((rows, spread), jnp.float32)
        for k in range(routes_ref.shape[2]):
            named = routes_ref[b, :, k : k + 1] == expert_of
            dense = dense + jnp.where(named, gates_ref[b, :, k : k + 1], 0.0)
        high = dense.astype(jnp.bfloat16).astype(jnp.float32)
        tail = jnp.where(lane < experts, high, dense - high)
        tails.append(jnp.where(lane < 2 * experts, tail, 0.0))
    gathered[0:block, width:] = jnp.concatenate(tails, axis=0).astype(jnp.bfloat16)

    pl.semaphore_wait(barrier, len(others))

    def slot(far_core, far_side, step):
        start = ((far_core * PAIR + far_side) * ring + step) * block
        return pl.ds(pl.multiple_of(start, block), block)

    def gather_z(step):
        return remote(
            gathered.at[slot(0, 0, 0)],
            gathered.at[slot(0, 0, step)],
            gz_send.at[step],
            gz_recv.at[step],
            up_by(step),
        )

    def gather_x(step):
        return remote(
            gathered.at[slot(0, 0, step)],
            gathered.at[slot(0, 1, step)],
            gx_send.at[step],
            gx_recv.at[step],
            side,
        )

    def gather_c(far_side, step):
        return remote(
            gathered.at[slot(0, far_side, step)],
            gathered.at[slot(1, far_side, step)],
            gc_send.at[far_side * ring + step],
            gc_recv.at[far_side * ring + step],
            mate,
        )

    order = sorted(range(1, ring), key=lambda step: min(step, ring - step))
    for step in order:
        gather_z(step).start()
    gather_x(0).start()
    gather_c(0, 0).start()

    for load in loads[3:8]:
        load.wait()
    own_keys[...] = fresh_key_ref[...].astype(jnp.float32)
    own_values[...] = fresh_value_ref[...].astype(jnp.float32)
    for h in range(heads):
        q_rows[h * block : (h + 1) * block, :] = query_ref[
            :, h * HEAD_SIZE : (h + 1) * HEAD_SIZE
        ].astype(jnp.float32)

    head = lax.broadcasted_iota(jnp.int32, (heads, kv_heads * slots), 0)
    column = lax.broadcasted_iota(jnp.int32, (heads, kv_heads * slots), 1)
    position = jnp.where(head // group == column // slots, lax.rem(column, slots), slots)

    def grouped(ref, row):
        parts = [ref[row : row + 1, g * HEAD_SIZE : (g + 1) * HEAD_SIZE] for g in range(kv_heads)]
        return jnp.concatenate(
            [jnp.broadcast_to(part, (group, HEAD_SIZE)) for part in parts], axis=0
        )

    def stacked(ref, b, r):
        return jnp.concatenate(
            [ref[b, r, :, g * HEAD_SIZE : (g + 1) * HEAD_SIZE] for g in range(kv_heads)], axis=0
        )

    def attend(row):
        b, r = divmod(row, rows)
        picked = pl.ds(row, heads, stride=block)
        q = q_rows[picked, :]
        score = lax.dot_general(
            q.astype(jnp.bfloat16),
            stacked(keys, b, r),
            (((1,), (1,)), ((), ())),
            preferred_element_type=jnp.float32,
        )
        score = jnp.where(position < lengths_ref[b, r], score * scale, -jnp.inf)
        own_score = jnp.sum(q * grouped(own_keys, row), axis=1, keepdims=True) * scale
        top = jnp.maximum(jnp.max(score, axis=1, keepdims=True), own_score)
        raised = jnp.exp(score - top)
        own_raised = jnp.exp(own_score - top)
        share = 1.0 / (jnp.sum(raised, axis=1, keepdims=True) + own_raised)
        probs = (raised * share).astype(jnp.bfloat16)
        own_prob = (own_raised * share).astype(jnp.bfloat16).astype(jnp.float32)
        out = jnp.dot(probs, stacked(values, b, r), preferred_element_type=jnp.float32)
        o_rows[picked, :] = out + own_prob * grouped(own_values, row)

    todo = list(range(block))

    def attend_some(count):
        for _ in range(min(count, len(todo))):
            attend(todo.pop(0))

    attend_some(2)
    for step in order:
        gather_z(step).wait_recv()
        gather_x(step).start()
        gather_c(0, step).start()
        attend_some(2)
    for step in [0] + order:
        gather_x(step).wait_recv()
        gather_c(1, step).start()

    expert = me // PAIR

    def hidden_units(far_core):
        span = pl.ds(far_core * half, half)
        x = gathered[span, 0:width]
        gate_val = jnp.dot(x, w_gate[0], preferred_element_type=jnp.float32)
        up_val = jnp.dot(x, w_up[0], preferred_element_type=jnp.float32)
        act[span, :] = (gate_val / (1.0 + jnp.exp(-gate_val)) * up_val).astype(jnp.bfloat16)
        tail = gathered[span, width:].astype(jnp.float32)
        at = lax.broadcasted_iota(jnp.int32, tail.shape, 1)
        mine = jnp.sum(jnp.where(lax.rem(at, experts) == expert, tail, 0.0), axis=1, keepdims=True)
        row_weight[span, :] = jnp.broadcast_to(mine, (half, LANES))

    loads[8].wait()
    loads[9].wait()
    hidden_units(0)
    for far_side in range(PAIR):
        for step in range(ring):
            gather_c(far_side, step).wait_recv()
    hidden_units(1)
    loads[10].wait()

    def reduce_c(j):
        return remote(send_c.at[j], recv_c.at[j], rc_send.at[j], rc_recv.at[j], mate)

    def reduce_x(j):
        return remote(send_x.at[j], recv_x.at[j], rx_send.at[j], rx_recv.at[j], side)

    def reduce_z(j, step):
        at = j * ring + step
        return remote(
            send_z.at[j, step], recv_z.at[j, step], rz_send.at[at], rz_recv.at[at], down_by(step)
        )

    def project(j):
        columns = slice(j * chunk, (j + 1) * chunk)
        for far_core in (1, 0):
            span = pl.ds(far_core * half, half)
            out = jnp.dot(act[span, :], w_down[0, :, columns], preferred_element_type=jnp.float32)
            out = out * jnp.concatenate([row_weight[span, :]] * (chunk // LANES), axis=1)
            if far_core:
                send_c[j] = out.astype(jnp.bfloat16)
                reduce_c(j).start()
            else:
                keep_c[j] = out

    def after_c(j):
        reduce_c(j).wait_recv()
        for far_side in (1, 0):
            span = slice(far_side * quarter, (far_side + 1) * quarter)
            out = keep_c[j, span, :] + recv_c[j, span, :].astype(jnp.float32)
            if far_side:
                send_x[j] = out.astype(jnp.bfloat16)
                reduce_x(j).start()
            else:
                keep_x[j] = out

    def after_x(j):
        reduce_x(j).wait_recv()
        for step in order + [0]:
            span = slice(step * block, (step + 1) * block)
            out = keep_x[j, span, :] + recv_x[j, span, :].astype(jnp.float32)
            if step:
                send_z[j, step] = out.astype(jnp.bfloat16)
                reduce_z(j, step).start()
            else:
                keep_x[j, span, :] = out

    def after_z(j):
        out = keep_x[j, 0:block, :]
        for step in order:
            reduce_z(j, step).wait_recv()
            out = out + recv_z[j, step].astype(jnp.float32)
        moe_ref[:, j * chunk : (j + 1) * chunk] = out.astype(jnp.bfloat16)

    for tick in range(chunks + 2):
        if tick < chunks:
            project(tick)
        if tick >= 2:
            after_c(tick - 2)
    attend_some(4)
    for j in range(chunks):
        after_x(j)
        if j == 0:
            attend_some(4)
    attend_some(block)
    for h in range(heads):
        attn_ref[:, h * HEAD_SIZE : (h + 1) * HEAD_SIZE] = o_rows[
            h * block : (h + 1) * block, :
        ].astype(jnp.bfloat16)
    store_attn = pltpu.make_async_copy(attn_ref, attn_hbm, load_sems.at[11])
    store_attn.start()
    for j in range(chunks):
        after_z(j)
    store_moe = pltpu.make_async_copy(moe_ref, moe_hbm, load_sems.at[12])
    store_moe.start()

    for step in order:
        gather_z(step).wait_send()
    for step in range(ring):
        gather_x(step).wait_send()
        for far_side in range(PAIR):
            gather_c(far_side, step).wait_send()
    for j in range(chunks):
        reduce_c(j).wait_send()
        reduce_x(j).wait_send()
        for step in order:
            reduce_z(j, step).wait_send()
    store_attn.wait()
    store_moe.wait()


def finish_kernel(attn_in, moe_in, attn_out, moe_out):
    attn_out[...] = attn_in[...]
    moe_out[...] = moe_in[...]


def finished(attn_out, moe_out):
    vmem = pl.BlockSpec(memory_space=pltpu.VMEM)
    return pl.pallas_call(
        finish_kernel,
        out_shape=(
            jax.ShapeDtypeStruct(attn_out.shape, attn_out.dtype),
            jax.ShapeDtypeStruct(moe_out.shape, moe_out.dtype),
        ),
        in_specs=[vmem, vmem],
        out_specs=(vmem, vmem),
        compiler_params=pltpu.CompilerParams(vmem_limit_bytes=63 * 1024 * 1024),
    )(attn_out, moe_out)


def dense_shards(
    hidden_in,
    routes,
    gates,
    query,
    cached_key_rows,
    cached_value_rows,
    fresh_key,
    fresh_value,
    lengths,
    w_gate,
    w_up,
    w_down,
):
    ep_size = lax.axis_size("ep")
    experts = ep_size // PAIR
    ring = ep_size // (PAIR * PAIR)
    batches, rows, width = hidden_in.shape
    slots = cached_key_rows.shape[2]
    kv_heads = cached_key_rows.shape[3] // HEAD_SIZE
    heads = query.shape[2] // HEAD_SIZE
    depth = w_gate.shape[2]
    chunks = 4
    chunk = width // chunks
    block = batches * rows
    quarter = ring * block
    half = PAIR * quarter
    spread = -(-2 * experts // LANES) * LANES
    dims = (batches, rows, width, heads, kv_heads, slots, experts, depth, chunks, chunk)
    smem = pl.BlockSpec(memory_space=pltpu.SMEM)
    hbm = pl.BlockSpec(memory_space=pl.ANY)
    bf16, f32 = jnp.bfloat16, jnp.float32
    dma = pltpu.SemaphoreType.DMA
    def flat(array):
        return array.reshape(block, array.shape[2])

    attn_out, moe_out = pl.pallas_call(
        functools.partial(layer_kernel, dims),
        out_shape=(
            jax.ShapeDtypeStruct((block, query.shape[2]), bf16),
            jax.ShapeDtypeStruct((block, width), bf16),
        ),
        in_specs=[smem] + [hbm] * 11,
        out_specs=(hbm, hbm),
        scratch_shapes=[
            pltpu.VMEM((block, query.shape[2]), bf16),
            pltpu.VMEM((block, width), bf16),
            pltpu.VMEM((block, width), bf16),
            pltpu.VMEM(routes.shape, jnp.int32),
            pltpu.VMEM(gates.shape, f32),
            pltpu.VMEM((block, query.shape[2]), bf16),
            pltpu.VMEM((block, fresh_key.shape[2]), bf16),
            pltpu.VMEM((block, fresh_value.shape[2]), bf16),
            pltpu.VMEM(cached_key_rows.shape, bf16),
            pltpu.VMEM(cached_value_rows.shape, bf16),
            pltpu.VMEM(w_gate.shape, bf16),
            pltpu.VMEM(w_up.shape, bf16),
            pltpu.VMEM(w_down.shape, bf16),
            pltpu.VMEM((PAIR * half, width + spread), bf16),
            pltpu.VMEM((heads * block, HEAD_SIZE), f32),
            pltpu.VMEM((heads * block, HEAD_SIZE), f32),
            pltpu.VMEM((block, fresh_key.shape[2]), f32),
            pltpu.VMEM((block, fresh_value.shape[2]), f32),
            pltpu.VMEM((PAIR * half, LANES), f32),
            pltpu.VMEM((PAIR * half, depth), bf16),
            pltpu.VMEM((chunks, half, chunk), f32),
            pltpu.VMEM((chunks, quarter, chunk), f32),
            pltpu.VMEM((chunks, half, chunk), bf16),
            pltpu.VMEM((chunks, half, chunk), bf16),
            pltpu.VMEM((chunks, quarter, chunk), bf16),
            pltpu.VMEM((chunks, quarter, chunk), bf16),
            pltpu.VMEM((chunks, ring, block, chunk), bf16),
            pltpu.VMEM((chunks, ring, block, chunk), bf16),
            dma((13,)),
            dma((ring,)),
            dma((ring,)),
            dma((ring,)),
            dma((ring,)),
            dma((PAIR * ring,)),
            dma((PAIR * ring,)),
            dma((chunks,)),
            dma((chunks,)),
            dma((chunks,)),
            dma((chunks,)),
            dma((chunks * ring,)),
            dma((chunks * ring,)),
        ],
        compiler_params=pltpu.CompilerParams(
            collective_id=0, has_side_effects=True, vmem_limit_bytes=63 * 1024 * 1024
        ),
        cost_estimate=pl.CostEstimate(
            flops=6 * PAIR * half * width * depth, bytes_accessed=8 * 1024 * 1024, transcendentals=0
        ),
    )(
        lengths,
        flat(hidden_in),
        routes,
        gates,
        flat(query),
        flat(fresh_key),
        flat(fresh_value),
        cached_key_rows,
        cached_value_rows,
        w_gate,
        w_up,
        w_down,
    )
    attn_out, moe_out = finished(attn_out, moe_out)
    return attn_out.reshape(query.shape), moe_out.reshape(hidden_in.shape)


def shards(*args):
    hidden_in, routes = args[0], args[1]
    ep_size = lax.axis_size("ep")
    batches, rows, width = hidden_in.shape
    every_expert = routes.shape[2] == ep_size // PAIR
    fits = ep_size % (PAIR * PAIR) == 0 and ep_size > PAIR * PAIR and lax.axis_size("tp") == 1
    tiles = batches * rows % TILE_ROWS == 0 and rows % 8 == 0 and width % (8 * LANES) == 0
    if every_expert and fits and tiles:
        return dense_shards(*args)
    return sparse_shards(*args)


def solution(mesh):
    in_specs = (
        P(None, ("grp", "ep"), None),
        P(None, ("grp", "ep"), None),
        P(None, ("grp", "ep"), None),
        P(None, ("grp", "ep"), "tp"),
        P(None, ("grp", "ep"), None, "tp"),
        P(None, ("grp", "ep"), None, "tp"),
        P(None, ("grp", "ep"), "tp"),
        P(None, ("grp", "ep"), "tp"),
        P(None, ("grp", "ep")),
        P("ep", None, "tp"),
        P("ep", None, "tp"),
        P("ep", "tp", None),
    )
    out_specs = (P(None, ("grp", "ep"), "tp"), P(None, ("grp", "ep"), "tp"))
    return jax.shard_map(shards, mesh=mesh, in_specs=in_specs, out_specs=out_specs, check_vma=False)
```
